256 devices in a mesh: gx: 16 (over z, core), gy: 16 (over x, y).
Axes of the slice: x: 4, y: 4, z: 8, core: 2. Of those that a mesh axis runs over, the one named last changes fastest.
Arguments:
- velocity: float32 [3, 8192, 8192], P(None, 'gx', 'gy'), may hold values from -6 to 6
- metric_first: float32 [8192], P('gy'), may hold values from 0.5 to 2
- metric_second: float32 [8192], P('gy'), may hold values from -4 to 4
Outputs:
- increment: float32 [3, 8192, 8192], P(None, 'gx', 'gy')
The draws below stay inside these ranges and needn't reach their ends.
All inputs are finite; a program needn't handle non-finite values.
Results may differ from the reference program's by a relative error of at most 0.0003.
Values sent between devices are 32-bit elements; how exact they have to be, the bound alone decides.
No kernel may reach another device: no remote copies, remote signals or barrier semaphores. Data moves between devices by JAX's collectives and lax.ppermute only.
A program may use at most 128 MiB of HBM per device.

```python
import math
import jax
import jax.numpy as jnp
from jax import lax

NX = 8192
NY = 8192


def levels(rng, shape, pieces, least, top_value):
    gain, own = 1.0, jax.random.fold_in(rng, 6)
    for dim, parts in pieces:
        steps = jnp.exp(jax.random.uniform(jax.random.fold_in(own, dim), (parts,), jnp.float32, least / len(pieces), top_value / len(pieces)))
        gain = gain * jnp.repeat(steps, shape[dim] // parts).reshape([-1 if axis == dim else 1 for axis in range(len(shape))])
    return gain


def centred(own_key, extent, scale, reach, pieces=(), kind=jnp.bfloat16):
    entries = scale * jax.random.normal(own_key, extent, jnp.float32)
    if pieces:
        entries = entries * levels(own_key, extent, pieces, -0.22, 0.18)
    return jnp.clip(entries, -reach, reach).astype(kind)


def setup_inputs(seed: int = 0) -> dict:
    key_list = jax.random.split(jax.random.key(seed), 4)
    return {
        "velocity": centred(key_list[0], (3, NX, NY), 1.0, 6.0, ((1, 16), (2, 16)), jnp.float32),
        "metric_first": jnp.clip(jnp.exp(math.log(2.0) - 1.3862944 * jax.random.uniform(key_list[1], (NY,), jnp.float32) ** levels(key_list[1], (NY,), ((0, 16),), -0.2, 0.2)), 0.5, 2.0),
        "metric_second": centred(key_list[2], (NY,), 1.0, 4.0, ((0, 16),), jnp.float32),
    }


VISCOSITY = 0.2
DIFFUSION = 1.0

def stencils(field, ahead):
    first_rhs = (45.0 * (ahead(1) - ahead(-1)) - 9.0 * (ahead(2) - ahead(-2)) + (ahead(3) - ahead(-3))) / 60.0
    second_rhs = (270.0 * (ahead(1) + ahead(-1)) - 27.0 * (ahead(2) + ahead(-2)) + 2.0 * (ahead(3) + ahead(-3)) - 490.0 * field) / 180.0
    return (first_rhs, second_rhs)

def coefficients(cells):
    sigma = cells / 4.0
    diag = 1.0 + 2.0 * DIFFUSION + sigma
    return (-(DIFFUSION + sigma) / diag, -DIFFUSION / diag, diag, sigma)

def solve_tridiag(below, main, above, right_side, periodic):
    length = right_side.shape[0]
    wrap_low = below[0]
    wrap_up = above[-1]
    lower_band = below.at[0].set(0.0)
    upper_band = above.at[-1].set(0.0)
    if not periodic:
        return lax.linalg.tridiagonal_solve(lower_band, main, upper_band, right_side)
    gamma = -main[0]
    shifted = main.at[0].set(main[0] - gamma).at[-1].set(main[-1] - wrap_up * wrap_low / gamma)
    plain_sol = lax.linalg.tridiagonal_solve(lower_band, shifted, upper_band, right_side)
    corner_col = jnp.zeros((length, 1), right_side.dtype).at[0, 0].set(gamma).at[-1, 0].set(wrap_up)
    column_sol = lax.linalg.tridiagonal_solve(lower_band, shifted, upper_band, corner_col)
    weight = wrap_low / gamma
    factor = (plain_sol[0] + weight * plain_sol[-1]) / (1.0 + column_sol[0, 0] + weight * column_sol[-1, 0])
    return plain_sol - column_sol * factor[None, :]

def along_axis(field_stack, axis, lower, upper, periodic):
    along_lines = jnp.moveaxis(field_stack, axis, 0)
    line_shape = along_lines.shape
    ones = jnp.ones((line_shape[0],), field_stack.dtype)
    solved = solve_tridiag(lower * ones, ones, upper * ones, along_lines.reshape(line_shape[0], -1), periodic)
    return jnp.moveaxis(solved.reshape(line_shape), 0, axis)

def reference(velocity, metric_first, metric_second):
    low_x, up_x, diag_x, sig_x = coefficients(NX)
    low_y, up_y, diag_y, sig_y = coefficients(NY)
    first_x, second_x = stencils(velocity, lambda steps: jnp.roll(velocity, -steps, axis=1))
    padded = jnp.pad(velocity, ((0, 0), (0, 0), (3, 3)))
    first_eta, second_eta = stencils(velocity, lambda steps: padded[:, :, 3 + steps:3 + steps + NY])
    slope_y = metric_first * first_eta
    curve_y = metric_first * metric_first * second_eta + metric_second * first_eta
    tendency = -(velocity[0:1] * first_x + velocity[1:2] * slope_y) + VISCOSITY * (second_x + curve_y)
    right_side = tendency * (math.sqrt(sig_x * sig_y) / diag_x)
    half = along_axis(right_side, 1, low_x, up_x, True)
    return along_axis(half / diag_y, 2, low_y, up_y, False)
```

```python
import functools
import math

import jax
import jax.numpy as jnp
import numpy as np
from jax import lax
from jax.experimental import pallas as pl
from jax.experimental.pallas import tpu as pltpu
from jax.sharding import PartitionSpec as P

VISCOSITY = 0.2
DIFFUSION = 1.0
FIRST = (45.0 / 60.0, -9.0 / 60.0, 1.0 / 60.0)
SECOND = (270.0 / 180.0, -27.0 / 180.0, 2.0 / 180.0)
CENTRE = -490.0 / 180.0
ROWS = 64
F32 = jnp.float32
BF16 = jnp.bfloat16
VMEM_LIMIT = 48 * 1024 * 1024


def coefficients(cells):
    sigma = cells / 4.0
    diag = 1.0 + 2.0 * DIFFUSION + sigma
    return (-(DIFFUSION + sigma) / diag, -DIFFUSION / diag, diag, sigma)


def line_tables(length, lower, upper, blocks, periodic):
    matrix = np.eye(length) + lower * np.eye(length, k=-1) + upper * np.eye(length, k=1)
    inverse = np.linalg.inv(matrix)
    head = -lower * inverse[:, 0]
    tail = -upper * inverse[:, -1]
    order = 2 * blocks
    before = np.zeros((blocks, order))
    after = np.zeros((blocks, order))
    for block in range(blocks):
        if periodic or block > 0:
            before[block, 2 * ((block - 1) % blocks) + 1] = 1.0
        if periodic or block < blocks - 1:
            after[block, 2 * ((block + 1) % blocks)] = 1.0
    system = np.eye(order)
    for block in range(blocks):
        system[2 * block] -= head[0] * before[block] + tail[0] * after[block]
        system[2 * block + 1] -= head[-1] * before[block] + tail[-1] * after[block]
    solved = np.linalg.inv(system)
    sides = np.stack([before @ solved, after @ solved], axis=1)
    sides = sides.reshape(blocks, 2, blocks, 2).transpose(0, 2, 1, 3)
    return inverse, head, tail, sides


def split(values):
    high = values.astype(BF16)
    return high, (values - high.astype(F32)).astype(BF16)


def split_table(table):
    high = np.asarray(table, np.float32).astype(BF16)
    low = (np.asarray(table, np.float64) - high.astype(np.float64)).astype(BF16)
    return np.stack([high, low])


def dot3(left, right, dims):
    (lh, ll), (rh, rl) = left, right
    dot = functools.partial(
        lax.dot_general, dimension_numbers=(dims, ((), ())), preferred_element_type=F32
    )
    return dot(lh, rh) + (dot(lh, rl) + dot(ll, rh))


def padded_rows(rows, count):
    return jnp.concatenate(
        rows + [jnp.zeros((count - len(rows), rows[0].shape[1]), F32)], axis=0
    )


def edges_kernel(top, bottom, left, right, x_head, x_tail, y_head, y_tail, columns):
    for comp in range(3):
        x_head[3 * comp : 3 * comp + 3, :] = top[comp, 0:3, :]
        x_tail[3 * comp : 3 * comp + 3, :] = bottom[comp, 5:8, :]
    x_head[9:16, :] = jnp.zeros((7, x_head.shape[1]), F32)
    x_tail[9:16, :] = jnp.zeros((7, x_tail.shape[1]), F32)
    lane = lax.broadcasted_iota(jnp.int32, (64, 128), 1)
    for at in range(0, left.shape[1], 64):
        packed = jnp.zeros((64, 128), F32)
        for comp in range(3):
            here = pltpu.roll(left[comp, at : at + 64, :], 3 * comp, 1) if comp else left[comp, at : at + 64, :]
            packed = jnp.where((lane >= 3 * comp) & (lane < 3 * comp + 3), here, packed)
            here = pltpu.roll(right[comp, at : at + 64, :], 19 + 3 * comp, 1)
            packed = jnp.where((lane >= 16 + 3 * comp) & (lane < 19 + 3 * comp), here, packed)
        columns[at : at + 64, :] = packed
    for at in range(0, left.shape[1], 128):
        turned = columns[at : at + 128, :].T
        y_head[:, at : at + 128] = turned[0:16, :]
        y_tail[:, at : at + 128] = turned[16:32, :]


def inner_kernel(scale, above, own, below, m1, m2, ends_y, inner, ends, ext, columns):
    step = pl.program_id(0)
    last = pl.num_programs(0) - 1
    cells = own.shape[2]
    ext[:, 0:8, :] = jnp.where(step > 0, above[...], 0.0)
    ext[:, 8 : 8 + ROWS, :] = own[...]
    ext[:, 8 + ROWS : 16 + ROWS, :] = jnp.where(step < last, below[...], 0.0)
    first_row = m1[...]
    place = lax.broadcasted_iota(jnp.int32, (1, cells), 1)
    slope = scale * first_row
    offset = (scale * VISCOSITY) * m2[...]
    curve = (scale * VISCOSITY) * first_row * first_row
    middle = CENTRE * (curve + scale * VISCOSITY)
    lane = lax.broadcasted_iota(jnp.int32, (8, 128), 1)
    for at in range(0, ROWS, 8):
        rows = slice(8 + at, 16 + at)
        bend = offset - ext[1, rows, :] * slope
        along = ext[0, rows, :] * scale
        fields = [ext[comp, rows, :] for comp in range(3)]
        totals = [middle * field for field in fields]
        for k in (1, 2, 3):
            lead = FIRST[k - 1] * along
            x_ahead = (scale * VISCOSITY * SECOND[k - 1]) - lead
            x_behind = (scale * VISCOSITY * SECOND[k - 1]) + lead
            ahead = place < cells - k
            behind = place >= k
            bow = SECOND[k - 1] * curve
            y_ahead = jnp.where(ahead, bow, 0.0) + bend * jnp.where(ahead, FIRST[k - 1], 0.0)
            y_behind = jnp.where(behind, bow, 0.0) - bend * jnp.where(behind, FIRST[k - 1], 0.0)
            for comp in range(3):
                totals[comp] = (
                    totals[comp]
                    + (x_ahead * ext[comp, 8 + at + k : 16 + at + k, :] + x_behind * ext[comp, 8 + at - k : 16 + at - k, :])
                    + (y_ahead * pltpu.roll(fields[comp], cells - k, 1) + y_behind * pltpu.roll(fields[comp], k, 1))
                )
        packed = jnp.zeros((8, 128), F32)
        for comp in range(3):
            inner[comp, at : at + 8, :] = totals[comp]
            for end in (0, 1):
                value = jnp.sum(totals[comp] * ends_y[end : end + 1, :], axis=1, keepdims=True)
                packed = jnp.where(lane == 3 * end + comp, value, packed)
        columns[pl.ds(pl.multiple_of(step * ROWS + at, 8), 8), :] = packed

    @pl.when(step == last)
    def _():
        for at in range(0, columns.shape[0], 128):
            ends[:, at : at + 128] = columns[at : at + 128, :].T[0:8, :]


def weigh(table, index, other, values, swapped, third):
    base = 4 * other
    straight = jnp.where(third, table[index, base], table[index, base + 3])
    crossed = jnp.where(third, table[index, base + 1], table[index, base + 2])
    return straight * values + crossed * swapped


def swap_ends(values):
    return jnp.concatenate([values[3:6], values[0:3], values[6:8]], axis=0)


def halo_kernel(
    scale, blocks, index, table, before_x, after_x, before_y, after_y, x_head, x_tail, y_head, y_tail,
    m1, m2, ends_y, ends, shares, delta_x, delta_y,
):
    cells_x = before_y.shape[1]
    cells_y = before_x.shape[1]
    visc = scale * VISCOSITY
    x_rows = [[None] * 6 for _ in range(3)]
    y_rows = [[None] * 6 for _ in range(3)]
    for near in range(3):
        u_head = scale * x_head[near : near + 1, :]
        u_tail = scale * x_tail[2 - near : 3 - near, :]
        v_head = y_head[3 + near : 4 + near, :]
        v_tail = y_tail[5 - near : 6 - near, :]
        last = cells_y - 1 - near
        m1_head, m2_head = m1[0:1, near : near + 1], m2[0:1, near : near + 1]
        m1_tail, m2_tail = m1[0:1, last : last + 1], m2[0:1, last : last + 1]
        bend_head = visc * m2_head - v_head * (scale * m1_head)
        bend_tail = visc * m2_tail - v_tail * (scale * m1_tail)
        curve_head = visc * m1_head * m1_head
        curve_tail = visc * m1_tail * m1_tail
        for comp in range(3):
            x_low = x_high = y_low = y_high = None
            for k in range(near + 1, 4):
                a, b = FIRST[k - 1], SECOND[k - 1]
                low = 3 * comp + 3 + near - k
                high = 3 * comp + k - near - 1
                terms = (
                    (visc * b + a * u_head) * before_x[low : low + 1, :],
                    (visc * b - a * u_tail) * after_x[high : high + 1, :],
                    (b * curve_head - a * bend_head) * before_y[low : low + 1, :],
                    (b * curve_tail + a * bend_tail) * after_y[high : high + 1, :],
                )
                if x_low is None:
                    x_low, x_high, y_low, y_high = terms
                else:
                    x_low, x_high, y_low, y_high = (
                        x_low + terms[0], x_high + terms[1], y_low + terms[2], y_high + terms[3]
                    )
            x_rows[comp][near], x_rows[comp][5 - near] = x_low, x_high
            y_rows[comp][near], y_rows[comp][5 - near] = y_low, y_high
    zero_y = jnp.zeros((2, cells_y), F32)
    zero_x = jnp.zeros((2, cells_x), F32)
    for comp in range(3):
        delta_x[8 * comp : 8 * comp + 8, :] = jnp.concatenate(x_rows[comp] + [zero_y], axis=0)
        delta_y[8 * comp : 8 * comp + 8, :] = jnp.concatenate(y_rows[comp] + [zero_x], axis=0)
    row = lax.broadcasted_iota(jnp.int32, (8, 128), 0)
    lane = lax.broadcasted_iota(jnp.int32, (8, 128), 1)
    at_head = (row < 3) & (lane == row)
    at_tail = (row >= 3) & (row < 6) & (lane == row + 122)
    extra = [[], []]
    for comp in range(3):
        strip = delta_x[8 * comp : 8 * comp + 8, :]
        for end in (0, 1):
            value = jnp.sum(strip * ends_y[end : end + 1, :], axis=1, keepdims=True)
            total = jnp.concatenate(
                [
                    jnp.sum(jnp.where(at_head, value, 0.0), axis=0, keepdims=True),
                    jnp.zeros((1, cells_x - 256), F32),
                    jnp.sum(jnp.where(at_tail, value, 0.0), axis=0, keepdims=True),
                ],
                axis=1,
            )
            for j in range(3):
                last = cells_y - 1 - j
                total = total + (
                    y_rows[comp][j] * ends_y[end : end + 1, j : j + 1]
                    + y_rows[comp][5 - j] * ends_y[end : end + 1, last : last + 1]
                )
            extra[end].append(total)
    values = ends[...] + padded_rows(extra[0] + extra[1], 8)
    swapped = swap_ends(values)
    third = lax.broadcasted_iota(jnp.int32, (8, cells_x), 0) < 3
    for other in range(blocks):
        shares[other] = weigh(table, index[0], other, values, swapped, third)


def solve_kernel(inner, delta_x, delta_y, inverse_x, inverse_y, solved, edges, work, work2, columns):
    comp = pl.program_id(0)
    cells_x, cells_y = inner.shape[1], inner.shape[2]
    work[...] = inner[0]
    work[0:8, :] += jnp.concatenate([delta_x[0:3, :], jnp.zeros((5, cells_y), F32)], axis=0)
    work[cells_x - 8 : cells_x, :] += jnp.concatenate([jnp.zeros((5, cells_y), F32), delta_x[3:6, :]], axis=0)
    lane = lax.broadcasted_iota(jnp.int32, (128, 128), 1)
    for at in range(0, cells_x, 128):
        tile = jnp.concatenate([delta_y[:, at : at + 128], jnp.zeros((120, 128), F32)], axis=0).T
        work[at : at + 128, 0:128] += jnp.where(lane < 3, tile, 0.0)
        work[at : at + 128, cells_y - 128 : cells_y] += jnp.where(lane >= 125, pltpu.roll(tile, 122, 1), 0.0)
    right = (inverse_y[0], inverse_y[1])
    left = (inverse_x[0], inverse_x[1])
    half = cells_x // 2
    for at in (0, half):
        work2[at : at + half, :] = dot3(split(work[at : at + half, :]), right, ((1,), (1,)))
    for at in (0, half):
        lines = split(work2[:, at : at + half])
        solved[0, :, at : at + half] = dot3(left, lines, ((1,), (0,)))
    edges[pl.ds(comp, 1), :] = solved[0, 0:1, :]
    edges[pl.ds(comp + 3, 1), :] = solved[0, cells_x - 1 : cells_x, :]

    @pl.when(comp == 0)
    def _():
        edges[6:8, :] = jnp.zeros((2, cells_y), F32)


def ends_kernel(shares, edges, ends_x, sides_y, out, beside):
    total = shares[0]
    for block in range(1, shares.shape[0]):
        total = total + shares[block]
    beside[...] = total
    rows = []
    for end in (0, 1):
        value = jnp.sum(total * ends_x[end : end + 1, :], axis=1, keepdims=True)
        for comp in range(3):
            rows.append(
                value[comp : comp + 1] * sides_y[0:1, :] + value[comp + 3 : comp + 4] * sides_y[1:2, :]
            )
    out[...] = edges[...] + padded_rows(rows, 8)


def final_kernel(blocks, index, table, gathered, beside, inverse_x, sides_x, sides_y, solved, out, beyond, columns):
    step = pl.program_id(0)
    cells_x, cells_y = beside.shape[1], gathered.shape[2]

    @pl.when(step == 0)
    def _():
        third = lax.broadcasted_iota(jnp.int32, (8, cells_y), 0) < 3
        straight = jnp.zeros((8, cells_y), F32)
        crossed = jnp.zeros((8, cells_y), F32)
        for block in range(blocks):
            base = 4 * block
            values = gathered[block]
            straight += jnp.where(third, table[index[0], base], table[index[0], base + 3]) * values
            crossed += jnp.where(third, table[index[0], base + 2], table[index[0], base + 1]) * values
        beyond[...] = straight + swap_ends(crossed)
        lines = dot3(split(beside[...]), (inverse_x[0], inverse_x[1]), ((1,), (1,)))
        rows = jnp.concatenate([lines[0:6], sides_x[0:2], jnp.zeros((120, cells_x), F32)], axis=0)
        for at in range(0, cells_x, 128):
            columns[at : at + 128, :] = rows[:, at : at + 128].T

    for at in range(0, ROWS, 8):
        here = columns[pl.ds(pl.multiple_of(step * ROWS + at, 8), 8), :]
        head, tail = here[:, 6:7], here[:, 7:8]
        for comp in range(3):
            out[comp, at : at + 8, :] = (
                solved[comp, at : at + 8, :]
                + (here[:, comp : comp + 1] * sides_y[0:1, :] + here[:, comp + 3 : comp + 4] * sides_y[1:2, :])
                + (head * beyond[comp : comp + 1, :] + tail * beyond[comp + 3 : comp + 4, :])
            )


def whole(shape):
    return pl.BlockSpec(shape, lambda *_: (0,) * len(shape))


def call(kernel, grid, in_specs, out_specs, out_shape, scratch, flops, nbytes):
    return pl.pallas_call(
        kernel,
        grid=grid,
        in_specs=in_specs,
        out_specs=out_specs,
        out_shape=out_shape,
        scratch_shapes=scratch,
        compiler_params=pltpu.CompilerParams(vmem_limit_bytes=VMEM_LIMIT),
        cost_estimate=pl.CostEstimate(flops=flops, bytes_accessed=nbytes, transcendentals=0),
    )


def local(velocity, metric_first, metric_second):
    _, nx, ny = velocity.shape
    blocks_x, blocks_y = lax.axis_size("gx"), lax.axis_size("gy")
    low_x, up_x, diag_x, sig_x = coefficients(blocks_x * nx)
    low_y, up_y, diag_y, sig_y = coefficients(blocks_y * ny)
    scale = math.sqrt(sig_x * sig_y) / (diag_x * diag_y)
    inverse_x, head_x, tail_x, among_x = line_tables(nx, low_x, up_x, blocks_x, True)
    inverse_y, head_y, tail_y, among_y = line_tables(ny, low_y, up_y, blocks_y, False)
    table_x = jnp.asarray(among_x.reshape(blocks_x, 4 * blocks_x), F32)
    table_y = jnp.asarray(among_y.transpose(1, 0, 2, 3).reshape(blocks_y, 4 * blocks_y), F32)
    ends_x = jnp.asarray(np.stack([inverse_x[0], inverse_x[-1]]), F32)
    ends_y = jnp.asarray(np.stack([inverse_y[0], inverse_y[-1]]), F32)
    sides_x = jnp.asarray(np.stack([head_x, tail_x]), F32)
    sides_y = jnp.asarray(np.stack([head_y, tail_y]), F32)
    parts_x = jnp.asarray(split_table(inverse_x))
    parts_y = jnp.asarray(split_table(inverse_y))
    index_x = lax.axis_index("gx").astype(jnp.int32).reshape(1)
    index_y = lax.axis_index("gy").astype(jnp.int32).reshape(1)
    m1 = metric_first.reshape(1, ny)
    m2 = metric_second.reshape(1, ny)
    smem = pl.BlockSpec(memory_space=pltpu.SMEM)
    struct = jax.ShapeDtypeStruct
    field = struct((3, nx, ny), F32)

    with jax.named_scope("edges"):
        x_head, x_tail, y_head, y_tail = call(
            edges_kernel,
            (1,),
            [
                pl.BlockSpec((3, 8, ny), lambda i: (0, 0, 0)),
                pl.BlockSpec((3, 8, ny), lambda i: (0, nx // 8 - 1, 0)),
                pl.BlockSpec((3, nx, 128), lambda i: (0, 0, 0)),
                pl.BlockSpec((3, nx, 128), lambda i: (0, 0, ny // 128 - 1)),
            ],
            [whole((16, ny)), whole((16, ny)), whole((16, nx)), whole((16, nx))],
            [struct((16, ny), F32)] * 2 + [struct((16, nx), F32)] * 2,
            [pltpu.VMEM((nx, 128), F32)],
            10 * nx * 128,
            8 * 3 * nx * 128,
        )(velocity, velocity, velocity, velocity)
    with jax.named_scope("halos"):
        round_x = [(i, (i + 1) % blocks_x) for i in range(blocks_x)]
        along_y = [(i, i + 1) for i in range(blocks_y - 1)]
        before_y = lax.ppermute(y_tail, "gy", along_y)
        after_y = lax.ppermute(y_head, "gy", [(b, a) for a, b in along_y])
        before_x = lax.ppermute(x_tail, "gx", round_x)
        after_x = lax.ppermute(x_head, "gx", [(b, a) for a, b in round_x])
    with jax.named_scope("inner"):
        strips = ROWS // 8
        inner, ends = call(
            functools.partial(inner_kernel, scale),
            (nx // ROWS,),
            [
                pl.BlockSpec((3, 8, ny), lambda i: (0, jnp.maximum(i * strips - 1, 0), 0)),
                pl.BlockSpec((3, ROWS, ny), lambda i: (0, i, 0)),
                pl.BlockSpec((3, 8, ny), lambda i: (0, jnp.minimum((i + 1) * strips, nx // 8 - 1), 0)),
                whole((1, ny)),
                whole((1, ny)),
                whole((2, ny)),
            ],
            [pl.BlockSpec((3, ROWS, ny), lambda i: (0, i, 0)), whole((8, nx))],
            [field, struct((8, nx), F32)],
            [pltpu.VMEM((3, ROWS + 16, ny), F32), pltpu.VMEM((nx, 128), F32)],
            40 * 3 * nx * ny,
            8 * 3 * nx * ny,
        )(velocity, velocity, velocity, m1, m2, ends_y)
    with jax.named_scope("halo_part"):
        shares, delta_x, delta_y = call(
            functools.partial(halo_kernel, scale, blocks_y),
            (1,),
            [smem, smem]
            + [whole((16, ny))] * 2
            + [whole((16, nx))] * 2
            + [whole((16, ny))] * 2
            + [whole((16, nx))] * 2
            + [whole((1, ny)), whole((1, ny)), whole((2, ny)), whole((8, nx))],
            [whole((blocks_y, 8, nx)), whole((24, ny)), whole((24, nx))],
            [struct((blocks_y, 8, nx), F32), struct((24, ny), F32), struct((24, nx), F32)],
            [],
            1000 * nx,
            500 * nx,
        )(index_y, table_y, before_x, after_x, before_y, after_y, x_head, x_tail, y_head, y_tail, m1, m2, ends_y, ends)
    with jax.named_scope("across_y"):
        got_y = lax.all_to_all(shares, "gy", 0, 0, tiled=True)
    with jax.named_scope("solve"):
        solved, edges = call(
            solve_kernel,
            (3,),
            [
                pl.BlockSpec((1, nx, ny), lambda c: (c, 0, 0)),
                pl.BlockSpec((8, ny), lambda c: (c, 0)),
                pl.BlockSpec((8, nx), lambda c: (c, 0)),
                whole((2, nx, nx)),
                whole((2, ny, ny)),
            ],
            [pl.BlockSpec((1, nx, ny), lambda c: (c, 0, 0)), whole((8, ny))],
            [field, struct((8, ny), F32)],
            [pltpu.VMEM((nx, ny), F32), pltpu.VMEM((nx, ny), F32), pltpu.VMEM((nx, 128), F32)],
            3 * 6 * nx * ny * (nx + ny),
            8 * 3 * nx * ny,
        )(inner, delta_x, delta_y, parts_x, parts_y)
    with jax.named_scope("ends_x"):
        own_ends, beside = call(
            ends_kernel,
            (1,),
            [whole((blocks_y, 8, nx)), whole((8, ny)), whole((2, nx)), whole((2, ny))],
            [whole((8, ny)), whole((8, nx))],
            [struct((8, ny), F32), struct((8, nx), F32)],
            [],
            100 * nx,
            500 * nx,
        )(got_y, edges, ends_x, sides_y)
    with jax.named_scope("across_x"):
        gathered = lax.all_gather(own_ends, "gx", axis=0)
    with jax.named_scope("final"):
        return call(
            functools.partial(final_kernel, blocks_x),
            (nx // ROWS,),
            [
                smem,
                smem,
                whole((blocks_x, 8, ny)),
                whole((8, nx)),
                whole((2, nx, nx)),
                whole((2, nx)),
                whole((2, ny)),
                pl.BlockSpec((3, ROWS, ny), lambda i: (0, i, 0)),
            ],
            pl.BlockSpec((3, ROWS, ny), lambda i: (0, i, 0)),
            field,
            [pltpu.VMEM((8, ny), F32), pltpu.VMEM((nx, 128), F32)],
            8 * 3 * nx * ny,
            8 * 3 * nx * ny,
        )(index_x, table_x, gathered, beside, parts_x, sides_x, sides_y, solved)


def solution(mesh):
    in_specs = (P(None, "gx", "gy"), P("gy"), P("gy"))
    out_specs = P(None, "gx", "gy")
    return jax.shard_map(local, mesh=mesh, in_specs=in_specs, out_specs=out_specs, check_vma=False)
```

```python
import functools
import math

import jax
import jax.numpy as jnp
import numpy as np
from jax import lax
from jax.experimental import pallas as pl
from jax.experimental.pallas import tpu as pltpu
from jax.sharding import PartitionSpec as P

VISCOSITY = 0.2
DIFFUSION = 1.0
FIRST = (45.0 / 60.0, -9.0 / 60.0, 1.0 / 60.0)
SECOND = (270.0 / 180.0, -27.0 / 180.0, 2.0 / 180.0)
CENTRE = -490.0 / 180.0
CUTS = (0, 8, 24, 56, 64)
UNROLL = 8
F32 = jnp.float32
BF16 = jnp.bfloat16
VMEM_LIMIT = 24 * 1024 * 1024


def coefficients(cells):
    sigma = cells / 4.0
    diag = 1.0 + 2.0 * DIFFUSION + sigma
    return (-(DIFFUSION + sigma) / diag, -DIFFUSION / diag, diag, sigma)


def line_tables(length, lower, upper, blocks, periodic):
    matrix = np.eye(length) + lower * np.eye(length, k=-1) + upper * np.eye(length, k=1)
    inverse = np.linalg.inv(matrix)
    head = -lower * inverse[:, 0]
    tail = -upper * inverse[:, -1]
    order = 2 * blocks
    before = np.zeros((blocks, order))
    after = np.zeros((blocks, order))
    for block in range(blocks):
        if periodic or block > 0:
            before[block, 2 * ((block - 1) % blocks) + 1] = 1.0
        if periodic or block < blocks - 1:
            after[block, 2 * ((block + 1) % blocks)] = 1.0
    system = np.eye(order)
    for block in range(blocks):
        system[2 * block] -= head[0] * before[block] + tail[0] * after[block]
        system[2 * block + 1] -= head[-1] * before[block] + tail[-1] * after[block]
    solved = np.linalg.inv(system)
    sides = np.stack([before @ solved, after @ solved], axis=1)
    sides = sides.reshape(blocks, 2, blocks, 2).transpose(0, 2, 1, 3)
    return inverse, head, tail, sides


def split(values):
    high = values.astype(BF16)
    return high, (values - high.astype(F32)).astype(BF16)


def split_table(table, axis):
    high = np.asarray(table, np.float32).astype(BF16)
    low = (np.asarray(table, np.float64) - high.astype(np.float64)).astype(BF16)
    return np.concatenate([high, high, low], axis=axis)


def padded_rows(rows, count):
    filled = sum(row.shape[0] for row in rows)
    return jnp.concatenate(rows + [jnp.zeros((count - filled, rows[0].shape[1]), F32)], axis=0)


def lane_blocks(cells):
    return [slice(at, at + 128) for at in range(0, cells, 128)]


def edges_kernel(field, x_head, x_tail, y_head, y_tail, top, bottom, left, right, columns, sems):
    rows, cells = field.shape[1], field.shape[2]
    copies = [
        pltpu.make_async_copy(field.at[:, 0:8, :], top, sems.at[0]),
        pltpu.make_async_copy(field.at[:, rows - 8 : rows, :], bottom, sems.at[1]),
        pltpu.make_async_copy(field.at[:, :, 0:128], left, sems.at[2]),
        pltpu.make_async_copy(field.at[:, :, cells - 128 : cells], right, sems.at[3]),
    ]
    for copy in copies:
        copy.start()
    x_head[...] = jnp.zeros(x_head.shape, F32)
    x_tail[...] = jnp.zeros(x_tail.shape, F32)
    for copy in copies[:2]:
        copy.wait()
    for comp in range(3):
        x_head[3 * comp : 3 * comp + 3, :] = top[comp, 0:3, :]
        x_tail[3 * comp : 3 * comp + 3, :] = bottom[comp, 5:8, :]
    for copy in copies[2:]:
        copy.wait()
    edge_columns(left, right, y_head, y_tail, columns)


def edge_columns(left, right, y_head, y_tail, columns):
    cells_x = left.shape[1]
    lane = lax.broadcasted_iota(jnp.int32, (64, 128), 1)
    for at in range(0, cells_x, 64):
        packed = jnp.zeros((64, 128), F32)
        for comp in range(3):
            here = left[comp, at : at + 64, :]
            here = pltpu.roll(here, 3 * comp, 1) if comp else here
            packed = jnp.where((lane >= 3 * comp) & (lane < 3 * comp + 3), here, packed)
            here = pltpu.roll(right[comp, at : at + 64, :], 19 + 3 * comp, 1)
            packed = jnp.where((lane >= 16 + 3 * comp) & (lane < 19 + 3 * comp), here, packed)
        columns[at : at + 64, :] = packed
    for block in lane_blocks(cells_x):
        turned = columns[block, :].T
        y_head[:, block] = turned[0:16, :]
        y_tail[:, block] = turned[16:32, :]


def inner_kernel(scale, field, m1, m2, ends_y, inner, ends, padded, result, along_rows, sums, load_sems, store_sems):
    rows, cells = result.shape[1], result.shape[2]
    blocks = lane_blocks(cells)
    count = len(blocks)
    visc = scale * VISCOSITY
    zero = jnp.zeros((8, 128), F32)
    bounds = [rows * at // 64 for at in CUTS]
    spans = list(zip(bounds[:-1], bounds[1:]))
    loads = []
    for which, (first, final) in enumerate(spans):
        low, high = (first + 8 if first else 0), min(final + 8, rows)
        loads.append(
            [
                pltpu.make_async_copy(
                    field.at[:, low:high, block], padded.at[:, at, low + 8 : high + 8, :], load_sems.at[which, at]
                )
                for at, block in enumerate(blocks)
            ]
        )
    for group in loads:
        for copy in group:
            copy.start()
    for comp in range(3):
        for at in range(count):
            padded[comp, at, 0:8, :] = zero
            padded[comp, at, 8 + rows : 16 + rows, :] = zero
    slope = m1[...]
    curve = visc * slope * slope
    for at, row in enumerate(
        [scale * slope, visc * m2[...], SECOND[0] * curve, SECOND[1] * curve, SECOND[2] * curve]
        + [CENTRE * (curve + visc), ends_y[0:1, :], ends_y[1:2, :]]
    ):
        wide = jnp.broadcast_to(row, (8, cells))
        for place, block in enumerate(blocks):
            along_rows[at, place] = wide[:, block]
    lane = lax.broadcasted_iota(jnp.int32, (8, 128), 1)

    def step(index, carry):
        row = pl.multiple_of(index * 8, 8)
        fields = [[padded[comp, at, pl.ds(row + 8, 8), :] for at in range(count)] for comp in range(3)]
        along = [scale * part for part in fields[0]]
        bend = [along_rows[1, at] - fields[1][at] * along_rows[0, at] for at in range(count)]
        totals = [[along_rows[5, at] * fields[comp][at] for at in range(count)] for comp in range(3)]
        for k in (1, 2, 3):
            lead = [FIRST[k - 1] * part for part in along]
            lean = [FIRST[k - 1] * part for part in bend]
            x_ahead = [visc * SECOND[k - 1] - part for part in lead]
            x_behind = [visc * SECOND[k - 1] + part for part in lead]
            y_ahead = [along_rows[1 + k, at] + lean[at] for at in range(count)]
            y_behind = [along_rows[1 + k, at] - lean[at] for at in range(count)]
            for comp in range(3):
                left = [pltpu.roll(part, 128 - k, 1) for part in fields[comp]] + [zero]
                right = [zero] + [pltpu.roll(part, k, 1) for part in fields[comp]]
                for at in range(count):
                    totals[comp][at] = (
                        totals[comp][at]
                        + (
                            x_ahead[at] * padded[comp, at, pl.ds(row + 8 + k, 8), :]
                            + x_behind[at] * padded[comp, at, pl.ds(row + 8 - k, 8), :]
                        )
                        + (
                            y_ahead[at] * jnp.where(lane < 128 - k, left[at], left[at + 1])
                            + y_behind[at] * jnp.where(lane >= k, right[at + 1], right[at])
                        )
                    )
        for comp in range(3):
            for end in (0, 1):
                value = totals[comp][0] * along_rows[6 + end, 0]
                for at in range(1, count):
                    value = value + totals[comp][at] * along_rows[6 + end, at]
                sums[3 * end + comp, pl.ds(row, 8), :] = value
            for at, block in enumerate(blocks):
                result[comp, pl.ds(row, 8), block] = totals[comp][at]
        return carry

    stores = []
    for which, (first, final) in enumerate(spans):
        for copy in loads[which]:
            copy.wait()
        lax.fori_loop(first // 8, final // 8, step, 0, unroll=UNROLL)
        store = pltpu.make_async_copy(
            result.at[:, first:final, :], inner.at[:, first:final, :], store_sems.at[which]
        )
        store.start()
        stores.append(store)
    for block in lane_blocks(rows):
        values = [jnp.sum(sums[at, block, :].T, axis=0, keepdims=True) for at in range(6)]
        ends[:, block] = padded_rows(values, 8)
    for store in stores:
        store.wait()


def pack(values):
    return jnp.concatenate([values[0:6, block] for block in lane_blocks(values.shape[1])], axis=0)


def unpack(values):
    count = values.shape[0] // 6
    return jnp.concatenate([values[6 * at : 6 * at + 6, :] for at in range(count)], axis=1)


def write_shares(table, index, values, shares):
    swapped = pack(jnp.concatenate([values[3:6], values[0:3]], axis=0))
    values = pack(values)
    place = lax.broadcasted_iota(jnp.int32, values.shape, 0)
    third = jnp.zeros(values.shape, jnp.bool_)
    for at in range(0, values.shape[0], 6):
        third = third | ((place >= at) & (place < at + 3))
    for other in range(shares.shape[0]):
        base = 4 * other
        straight = jnp.where(third, table[index[0], base], table[index[0], base + 3])
        crossed = jnp.where(third, table[index[0], base + 1], table[index[0], base + 2])
        shares[other] = straight * values + crossed * swapped


def halo_sides(before, after, curves, bends_head, bends_tail):
    rows = lax.broadcasted_iota(jnp.int32, (16, 1), 0)
    line = rows - 3 * ((rows >= 3).astype(jnp.int32) + (rows >= 6).astype(jnp.int32))
    inside = rows < 9
    head = tail = None
    for k in (1, 2, 3):
        a, b = FIRST[k - 1], SECOND[k - 1]
        low = jnp.where(inside & (line < k), (b * curves[0] - a * bends_head), 0.0)
        high = jnp.where(inside & (line >= 3 - k), (b * curves[1] + a * bends_tail), 0.0)
        low = low * (pltpu.roll(before, 16 - (3 - k), 0) if k < 3 else before)
        high = high * (pltpu.roll(after, 3 - k, 0) if k < 3 else after)
        head = low if head is None else head + low
        tail = high if tail is None else tail + high
    return head, tail


def tiled_lines(lines):
    return jnp.concatenate([lines, lines, lines, jnp.zeros((7, lines.shape[1]), F32)], axis=0)


def line_column(row, first):
    rows = lax.broadcasted_iota(jnp.int32, (16, 1), 0)
    column = jnp.zeros((16, 1), F32)
    for at in range(9):
        column = jnp.where(rows == at, row[0:1, first + at % 3 : first + at % 3 + 1], column)
    return column


def halo_kernel(
    scale, index, table, before_x, after_x, before_y, after_y, x_head, x_tail, y_head, y_tail,
    m1, m2, ends_y, near_ends, ends, shares, delta_x, delta_y,
):
    cells_x = before_y.shape[1]
    cells_y = before_x.shape[1]
    visc = scale * VISCOSITY
    head_x, tail_x = halo_sides(
        before_x[...],
        after_x[...],
        (visc, visc),
        -scale * tiled_lines(x_head[0:3, :]),
        -scale * tiled_lines(x_tail[0:3, :]),
    )
    row1, row2 = m1[...], m2[...]
    ends_at = (0, cells_y - 3)
    slopes = [line_column(row1, at) for at in ends_at]
    offsets = [visc * line_column(row2, at) for at in ends_at]
    bends = [
        offsets[side] - (scale * slopes[side]) * tiled_lines(lines[3:6, :])
        for side, lines in enumerate((y_head, y_tail))
    ]
    head_y, tail_y = halo_sides(
        jnp.where(index[0] > 0, before_y[...], 0.0),
        jnp.where(index[0] < shares.shape[0] - 1, after_y[...], 0.0),
        [visc * slope * slope for slope in slopes],
        bends[0],
        bends[1],
    )
    delta_x[0:16, :] = head_x
    delta_x[16:32, :] = tail_x
    delta_y[0:16, :] = head_y
    delta_y[16:32, :] = tail_y
    values = ends[...] + lax.dot_general(
        near_ends[...],
        jnp.concatenate([head_y, tail_y], axis=0),
        (((1,), (0,)), ((), ())),
        precision=lax.Precision.HIGHEST,
        preferred_element_type=F32,
    )
    rows = lax.broadcasted_iota(jnp.int32, (16, 128), 0)
    line = rows - 3 * ((rows >= 3).astype(jnp.int32) + (rows >= 6).astype(jnp.int32))
    lane = lax.broadcasted_iota(jnp.int32, (16, 128), 1)
    extra = []
    for end in (0, 1):
        weights = ends_y[end : end + 1, :]
        first = jnp.sum(head_x * weights, axis=1, keepdims=True) * jnp.where(lane == line, 1.0, 0.0)
        final = jnp.sum(tail_x * weights, axis=1, keepdims=True) * jnp.where(lane == line + 125, 1.0, 0.0)
        for comp in range(3):
            own = (rows >= 3 * comp) & (rows < 3 * comp + 3)
            extra.append(
                jnp.concatenate(
                    [
                        jnp.sum(jnp.where(own, first, 0.0), axis=0, keepdims=True),
                        jnp.zeros((1, cells_x - 256), F32),
                        jnp.sum(jnp.where(own, final, 0.0), axis=0, keepdims=True),
                    ],
                    axis=1,
                )
            )
    write_shares(table, index, values + padded_rows(extra, 8), shares)


def turned_rows(rows, turned):
    tall = jnp.concatenate([rows, jnp.zeros((128 - rows.shape[0], rows.shape[1]), F32)], axis=0)
    for block in lane_blocks(rows.shape[1]):
        turned[block, :] = tall[:, block].T


def solve_y_kernel(
    inner, delta_x, delta_y, rows_x, table, lines, edges,
    work, result, inverse, turned, wide, sems,
):
    cells_x, cells = result.shape[1], result.shape[2]
    loads = [pltpu.make_async_copy(inner.at[comp], work.at[comp], sems.at[comp]) for comp in range(3)]
    tables = [pltpu.make_async_copy(table, inverse, sems.at[3])]
    for copy in loads[:1] + tables + loads[1:]:
        copy.start()
    turned_rows(rows_x[...], turned)
    for at in range(0, cells_x, 128):
        for end in (0, 1):
            wide[end, at : at + 128, :] = jnp.broadcast_to(turned[at : at + 128, end : end + 1], (128, 128))
    turned_rows(delta_y[...], turned)
    lane = lax.broadcasted_iota(jnp.int32, (128, 128), 1)
    found = [None] * 6
    half = cells_x // 2
    stores = []
    for comp in range(3):
        loads[comp].wait()
        for at in range(0, cells_x, 128):
            tile = turned[at : at + 128, :]
            near = pltpu.roll(tile, 128 - 3 * comp, 1) if comp else tile
            work[comp, at : at + 128, 0:128] += jnp.where(lane < 3, near, 0.0)
            far = pltpu.roll(tile, 109 - 3 * comp, 1)
            work[comp, at : at + 128, cells - 128 : cells] += jnp.where(lane >= 125, far, 0.0)
        work[comp, 0:3, :] += delta_x[3 * comp : 3 * comp + 3, :]
        work[comp, cells_x - 3 : cells_x, :] += delta_x[16 + 3 * comp : 19 + 3 * comp, :]
        if comp == 0:
            for copy in tables:
                copy.wait()
        for at in (0, half):
            high, low = split(work[comp, at : at + half, :])
            solved = jnp.dot(
                jnp.concatenate([high, low, high], axis=1), inverse[...], preferred_element_type=F32
            )
            result[comp, at : at + half, :] = solved
            for end in (0, 1):
                weights = wide[end, at : at + half, :]
                value = jnp.concatenate(
                    [
                        jnp.sum((solved[:, lanes] * weights).reshape(half // 8, 8, 128), axis=0)
                        for lanes in lane_blocks(cells)
                    ],
                    axis=1,
                )
                where = 3 * end + comp
                found[where] = value if found[where] is None else found[where] + value
        store = pltpu.make_async_copy(result.at[comp], lines.at[comp], sems.at[4 + comp])
        store.start()
        stores.append(store)
    edges[...] = padded_rows([jnp.sum(value, axis=0, keepdims=True) for value in found], 8)
    for store in stores:
        store.wait()


def ends_kernel(index, table, got, edges, ends_x, sides_y, shares, beside):
    total = got[0]
    for block in range(1, got.shape[0]):
        total = total + got[block]
    total = unpack(total)
    beside[...] = padded_rows([total], 8)
    rows = []
    for end in (0, 1):
        value = jnp.sum(total * ends_x[end : end + 1, :], axis=1, keepdims=True)
        for comp in range(3):
            rows.append(
                value[comp : comp + 1] * sides_y[0:1, :] + value[comp + 3 : comp + 4] * sides_y[1:2, :]
            )
    write_shares(table, index, edges[...] + padded_rows(rows, 8), shares)


def solve_x_kernel(lines, beside, sides_y, table, solved, work, inverse, turned, sems):
    cells_x, cells_y = solved.shape[1], solved.shape[2]
    tables = [pltpu.make_async_copy(table, inverse, sems.at[3])]
    loads = [pltpu.make_async_copy(lines.at[comp], work.at[comp], sems.at[comp]) for comp in range(3)]
    for copy in loads[:1] + tables + loads[1:]:
        copy.start()
    turned_rows(beside[...], turned)
    half = cells_y // 2
    before, after = sides_y[0:1, :], sides_y[1:2, :]
    for comp in range(3):
        loads[comp].wait()
        if comp == 0:
            for copy in tables:
                copy.wait()
        for at in (0, half):
            block = slice(at, at + half)
            full = (
                work[comp, :, block]
                + turned[:, comp : comp + 1] * before[:, block]
                + turned[:, comp + 3 : comp + 4] * after[:, block]
            )
            high, low = split(full)
            solved[comp, :, block] = jnp.dot(
                inverse[...], jnp.concatenate([high, low, high], axis=0), preferred_element_type=F32
            )


def final_kernel(got, rows_x, solved, out, beyond, turned):
    step = pl.program_id(0)
    rows = out.shape[1]
    blocks = lane_blocks(out.shape[2])

    @pl.when(step == 0)
    def _():
        turned_rows(rows_x[...], turned)
        total = got[0]
        for block in range(1, got.shape[0]):
            total = total + got[block]
        for row in range(6):
            for at in range(len(blocks)):
                beyond[row, at] = jnp.broadcast_to(total[6 * at + row : 6 * at + row + 1, :], (8, 128))

    for at in range(0, rows, 8):
        where = pl.ds(pl.multiple_of(step * rows + at, 8), 8)
        here = turned[where, :]
        head = jnp.broadcast_to(here[:, 2:3], (8, 128))
        tail = jnp.broadcast_to(here[:, 3:4], (8, 128))
        for comp in range(3):
            for place, block in enumerate(blocks):
                out[comp, at : at + 8, block] = solved[comp, where, block] + (
                    head * beyond[comp, place] + tail * beyond[comp + 3, place]
                )


VMEM = pl.BlockSpec(memory_space=pltpu.VMEM)
SMEM = pl.BlockSpec(memory_space=pltpu.SMEM)
HBM = pl.BlockSpec(memory_space=pltpu.HBM)


def in_hbm(values):
    return pltpu.with_memory_space_constraint(values, pltpu.HBM)


def struct(*shape):
    return jax.ShapeDtypeStruct(shape, F32)


def call(kernel, in_specs, out_shape, scratch, flops, nbytes, **kinds):
    if "out_specs" not in kinds:
        kinds["out_specs"] = [VMEM] * len(out_shape)
    return pl.pallas_call(
        kernel,
        in_specs=in_specs,
        out_shape=out_shape,
        scratch_shapes=scratch,
        compiler_params=pltpu.CompilerParams(vmem_limit_bytes=VMEM_LIMIT),
        cost_estimate=pl.CostEstimate(flops=flops, bytes_accessed=nbytes, transcendentals=0),
        **kinds,
    )


def local(velocity, metric_first, metric_second):
    _, nx, ny = velocity.shape
    blocks_x, blocks_y = lax.axis_size("gx"), lax.axis_size("gy")
    low_x, up_x, diag_x, sig_x = coefficients(blocks_x * nx)
    low_y, up_y, diag_y, sig_y = coefficients(blocks_y * ny)
    scale = math.sqrt(sig_x * sig_y) / (diag_x * diag_y)
    inverse_x, head_x, tail_x, among_x = line_tables(nx, low_x, up_x, blocks_x, True)
    inverse_y, head_y, tail_y, among_y = line_tables(ny, low_y, up_y, blocks_y, False)
    table_x = jnp.asarray(among_x.transpose(1, 0, 2, 3).reshape(blocks_x, 4 * blocks_x), F32)
    table_y = jnp.asarray(among_y.transpose(1, 0, 2, 3).reshape(blocks_y, 4 * blocks_y), F32)
    ends_x = jnp.asarray(np.stack([inverse_x[0], inverse_x[-1]]), F32)
    ends_y = jnp.asarray(np.stack([inverse_y[0], inverse_y[-1]]), F32)
    near = np.zeros((8, 32))
    for end, row in enumerate((inverse_y[0], inverse_y[-1])):
        for comp in range(3):
            near[3 * end + comp, 3 * comp : 3 * comp + 3] = row[:3]
            near[3 * end + comp, 16 + 3 * comp : 19 + 3 * comp] = row[-3:]
    near_ends = jnp.asarray(near, F32)
    rows_x = np.zeros((8, nx))
    rows_x[:4] = np.stack([inverse_x[0], inverse_x[-1], head_x, tail_x])
    rows_x = jnp.asarray(rows_x, F32)
    sides_y = jnp.asarray(np.stack([head_y, tail_y]), F32)
    parts_x = in_hbm(jnp.asarray(split_table(inverse_x, 1)))
    parts_y = in_hbm(jnp.asarray(split_table(inverse_y.T, 0)))
    index_x = lax.axis_index("gx").astype(jnp.int32).reshape(1)
    index_y = lax.axis_index("gy").astype(jnp.int32).reshape(1)
    m1 = metric_first.reshape(1, ny)
    m2 = metric_second.reshape(1, ny)
    cells = 3 * nx * ny
    round_x = [(i, (i + 1) % blocks_x) for i in range(blocks_x)]
    back_x = [(b, a) for a, b in round_x]
    round_y = [(i, (i + 1) % blocks_y) for i in range(blocks_y)]
    back_y = [(b, a) for a, b in round_y]

    velocity = in_hbm(velocity)
    with jax.named_scope("edges"):
        x_head, x_tail, y_head, y_tail = call(
            edges_kernel,
            [HBM],
            [struct(16, ny)] * 2 + [struct(16, nx)] * 2,
            [pltpu.VMEM((3, 8, ny), F32)] * 2
            + [pltpu.VMEM((3, nx, 128), F32)] * 2
            + [pltpu.VMEM((nx, 128), F32), pltpu.SemaphoreType.DMA((4,))],
            10 * nx * 128,
            24 * nx * 128,
        )(velocity)
    with jax.named_scope("halos"):
        before_x = lax.ppermute(x_tail, "gx", round_x)
        after_x = lax.ppermute(x_head, "gx", back_x)
        before_y = lax.ppermute(y_tail, "gy", round_y)
        after_y = lax.ppermute(y_head, "gy", back_y)
    with jax.named_scope("inner"):
        inner, ends = call(
            functools.partial(inner_kernel, scale),
            [HBM] + [VMEM] * 3,
            [pltpu.HBM((3, nx, ny), F32), struct(8, nx)],
            [
                pltpu.VMEM((3, ny // 128, nx + 16, 128), F32),
                pltpu.VMEM((3, nx, ny), F32),
                pltpu.VMEM((8, ny // 128, 8, 128), F32),
                pltpu.VMEM((6, nx, 128), F32),
                pltpu.SemaphoreType.DMA((len(CUTS) - 1, ny // 128)),
                pltpu.SemaphoreType.DMA((len(CUTS) - 1,)),
            ],
            40 * cells,
            8 * cells,
            out_specs=[HBM, VMEM],
        )(velocity, m1, m2, ends_y)
    with jax.named_scope("halo_part"):
        shares_y, delta_x, delta_y = call(
            functools.partial(halo_kernel, scale),
            [SMEM, SMEM] + [VMEM] * 13,
            [struct(blocks_y, 6 * (nx // 128), 128), struct(32, ny), struct(32, nx)],
            [],
            1000 * nx,
            500 * nx,
        )(
            index_y, table_y, before_x, after_x, before_y, after_y, x_head, x_tail, y_head, y_tail,
            m1, m2, ends_y, near_ends, ends,
        )
    with jax.named_scope("across_y"):
        got_y = lax.all_to_all(shares_y, "gy", 0, 0, tiled=True)
    with jax.named_scope("solve_y"):
        lines, edges = call(
            solve_y_kernel,
            [HBM] + [VMEM] * 3 + [HBM],
            [pltpu.HBM((3, nx, ny), F32), struct(8, ny)],
            [pltpu.VMEM((3, nx, ny), F32)] * 2
            + [pltpu.VMEM((3 * ny, ny), BF16), pltpu.VMEM((nx, 128), F32), pltpu.VMEM((2, nx, 128), F32)]
            + [pltpu.SemaphoreType.DMA((7,))],
            6 * cells * ny,
            8 * cells,
            out_specs=[HBM, VMEM],
        )(in_hbm(inner), delta_x, delta_y, rows_x, parts_y)
    with jax.named_scope("ends_x"):
        shares_x, beside = call(
            ends_kernel,
            [SMEM, SMEM] + [VMEM] * 4,
            [struct(blocks_x, 6 * (ny // 128), 128), struct(8, nx)],
            [],
            100 * nx,
            500 * nx,
        )(index_x, table_x, got_y, edges, ends_x, sides_y)
    with jax.named_scope("across_x"):
        got_x = lax.all_to_all(shares_x, "gx", 0, 0, tiled=True)
    with jax.named_scope("solve_x"):
        (solved,) = call(
            solve_x_kernel,
            [HBM, VMEM, VMEM, HBM],
            [struct(3, nx, ny)],
            [pltpu.VMEM((3, nx, ny), F32), pltpu.VMEM((nx, 3 * nx), BF16), pltpu.VMEM((nx, 128), F32)]
            + [pltpu.SemaphoreType.DMA((4,))],
            6 * cells * nx,
            8 * cells,
        )(in_hbm(lines), beside, sides_y, parts_x)
    with jax.named_scope("final"):
        return call(
            final_kernel,
            [VMEM] * 3,
            struct(3, nx, ny),
            [pltpu.VMEM((6, ny // 128, 8, 128), F32), pltpu.VMEM((nx, 128), F32)],
            4 * cells,
            8 * cells,
            grid=(nx // 128,),
            out_specs=pl.BlockSpec((3, 128, ny), lambda i: (0, i, 0)),
        )(got_x, rows_x, solved)


def solution(mesh):
    in_specs = (P(None, "gx", "gy"), P("gy"), P("gy"))
    out_specs = P(None, "gx", "gy")
    return jax.shard_map(local, mesh=mesh, in_specs=in_specs, out_specs=out_specs, check_vma=False)
```

```python
import functools
import math

import jax
import jax.numpy as jnp
import numpy as np
from jax import lax
from jax.experimental import pallas as pl
from jax.experimental.pallas import tpu as pltpu
from jax.sharding import PartitionSpec as P

VISCOSITY = 0.2
DIFFUSION = 1.0
FIRST = (45.0 / 60.0, -9.0 / 60.0, 1.0 / 60.0)
SECOND = (270.0 / 180.0, -27.0 / 180.0, 2.0 / 180.0)
CENTRE = -490.0 / 180.0
CUTS = (0, 8, 24, 56, 64)
UNROLL = 8
F32 = jnp.float32
BF16 = jnp.bfloat16
VMEM_LIMIT = 24 * 1024 * 1024


def coefficients(cells):
    sigma = cells / 4.0
    diag = 1.0 + 2.0 * DIFFUSION + sigma
    return (-(DIFFUSION + sigma) / diag, -DIFFUSION / diag, diag, sigma)


def line_tables(length, lower, upper, blocks, periodic):
    matrix = np.eye(length) + lower * np.eye(length, k=-1) + upper * np.eye(length, k=1)
    inverse = np.linalg.inv(matrix)
    head = -lower * inverse[:, 0]
    tail = -upper * inverse[:, -1]
    order = 2 * blocks
    before = np.zeros((blocks, order))
    after = np.zeros((blocks, order))
    for block in range(blocks):
        if periodic or block > 0:
            before[block, 2 * ((block - 1) % blocks) + 1] = 1.0
        if periodic or block < blocks - 1:
            after[block, 2 * ((block + 1) % blocks)] = 1.0
    system = np.eye(order)
    for block in range(blocks):
        system[2 * block] -= head[0] * before[block] + tail[0] * after[block]
        system[2 * block + 1] -= head[-1] * before[block] + tail[-1] * after[block]
    solved = np.linalg.inv(system)
    sides = np.stack([before @ solved, after @ solved], axis=1)
    sides = sides.reshape(blocks, 2, blocks, 2).transpose(0, 2, 1, 3)
    return inverse, head, tail, sides


def split(values):
    high = values.astype(BF16)
    return high, (values - high.astype(F32)).astype(BF16)


def split_table(table):
    high = np.asarray(table, np.float32).astype(BF16)
    low = (np.asarray(table, np.float64) - high.astype(np.float64)).astype(BF16)
    return np.stack([high, low])


def padded_rows(rows, count):
    filled = sum(row.shape[0] for row in rows)
    return jnp.concatenate(rows + [jnp.zeros((count - filled, rows[0].shape[1]), F32)], axis=0)


def lane_blocks(cells):
    return [slice(at, at + 128) for at in range(0, cells, 128)]


def edges_kernel(field, x_head, x_tail, y_head, y_tail, top, bottom, left, right, sems):
    rows, cells = field.shape[1], field.shape[2]
    ends = [
        pltpu.make_async_copy(field.at[:, 0:8, :], top, sems.at[0]),
        pltpu.make_async_copy(field.at[:, rows - 8 : rows, :], bottom, sems.at[1]),
    ]
    blocks = lane_blocks(rows)
    sides = [
        [
            pltpu.make_async_copy(field.at[:, block, 0:128], left.at[:, block, :], sems.at[2 + 2 * at]),
            pltpu.make_async_copy(field.at[:, block, cells - 128 : cells], right.at[:, block, :], sems.at[3 + 2 * at]),
        ]
        for at, block in enumerate(blocks)
    ]
    for group in sides + [ends]:
        for copy in group:
            copy.start()
    x_head[9:16, :] = jnp.zeros((7, cells), F32)
    x_tail[9:16, :] = jnp.zeros((7, cells), F32)
    lane = lax.broadcasted_iota(jnp.int32, (128, 128), 1)
    for group, block in zip(sides, blocks):
        for copy in group:
            copy.wait()
        packed = left[0, block, :]
        for comp in range(3):
            if comp:
                packed = jnp.where(lane < 3 * comp, packed, pltpu.roll(left[comp, block, :], 3 * comp, 1))
        packed = jnp.where(lane < 9, packed, 0.0)
        for comp in range(3):
            here = pltpu.roll(right[comp, block, :], 19 + 3 * comp, 1)
            packed = jnp.where((lane >= 16 + 3 * comp) & (lane < 19 + 3 * comp), here, packed)
        turned = packed.T
        y_head[:, block] = turned[0:16, :]
        y_tail[:, block] = turned[16:32, :]
    for copy in ends:
        copy.wait()
    for comp in range(3):
        x_head[3 * comp : 3 * comp + 3, :] = top[comp, 0:3, :]
        x_tail[3 * comp : 3 * comp + 3, :] = bottom[comp, 5:8, :]


def inner_kernel(scale, field, m1, m2, ends_y, inner, ends, padded, result, along_rows, sums, load_sems, store_sems):
    rows, cells = result.shape[1], result.shape[2]
    blocks = lane_blocks(cells)
    count = len(blocks)
    visc = scale * VISCOSITY
    zero = jnp.zeros((8, 128), F32)
    bounds = [rows * at // 64 for at in CUTS]
    spans = list(zip(bounds[:-1], bounds[1:]))
    loads = []
    for which, (first, final) in enumerate(spans):
        low, high = (first + 8 if first else 0), min(final + 8, rows)
        loads.append(
            [
                pltpu.make_async_copy(
                    field.at[:, low:high, block], padded.at[:, at, low + 8 : high + 8, :], load_sems.at[which, at]
                )
                for at, block in enumerate(blocks)
            ]
        )
    for group in loads:
        for copy in group:
            copy.start()
    for comp in range(3):
        for at in range(count):
            padded[comp, at, 0:8, :] = zero
            padded[comp, at, 8 + rows : 16 + rows, :] = zero
    slope = m1[...]
    curve = visc * slope * slope
    for at, row in enumerate(
        [scale * slope, visc * m2[...], SECOND[0] * curve, SECOND[1] * curve, SECOND[2] * curve]
        + [CENTRE * (curve + visc), ends_y[0:1, :], ends_y[1:2, :]]
    ):
        wide = jnp.broadcast_to(row, (8, cells))
        for place, block in enumerate(blocks):
            along_rows[at, place] = wide[:, block]
    lane = lax.broadcasted_iota(jnp.int32, (8, 128), 1)

    def step(index, carry):
        row = pl.multiple_of(index * 8, 8)
        fields = [[padded[comp, at, pl.ds(row + 8, 8), :] for at in range(count)] for comp in range(3)]
        along = [scale * part for part in fields[0]]
        bend = [along_rows[1, at] - fields[1][at] * along_rows[0, at] for at in range(count)]
        totals = [[along_rows[5, at] * fields[comp][at] for at in range(count)] for comp in range(3)]
        for k in (1, 2, 3):
            lead = [FIRST[k - 1] * part for part in along]
            lean = [FIRST[k - 1] * part for part in bend]
            x_ahead = [visc * SECOND[k - 1] - part for part in lead]
            x_behind = [visc * SECOND[k - 1] + part for part in lead]
            y_ahead = [along_rows[1 + k, at] + lean[at] for at in range(count)]
            y_behind = [along_rows[1 + k, at] - lean[at] for at in range(count)]
            for comp in range(3):
                left = [pltpu.roll(part, 128 - k, 1) for part in fields[comp]] + [zero]
                right = [zero] + [pltpu.roll(part, k, 1) for part in fields[comp]]
                for at in range(count):
                    totals[comp][at] = (
                        totals[comp][at]
                        + (
                            x_ahead[at] * padded[comp, at, pl.ds(row + 8 + k, 8), :]
                            + x_behind[at] * padded[comp, at, pl.ds(row + 8 - k, 8), :]
                        )
                        + (
                            y_ahead[at] * jnp.where(lane < 128 - k, left[at], left[at + 1])
                            + y_behind[at] * jnp.where(lane >= k, right[at + 1], right[at])
                        )
                    )
        for comp in range(3):
            for end in (0, 1):
                value = totals[comp][0] * along_rows[6 + end, 0]
                for at in range(1, count):
                    value = value + totals[comp][at] * along_rows[6 + end, at]
                sums[3 * end + comp, pl.ds(row, 8), :] = value
            for at, block in enumerate(blocks):
                result[comp, pl.ds(row, 8), block] = totals[comp][at]
        return carry

    stores = []
    for which, (first, final) in enumerate(spans):
        for copy in loads[which]:
            copy.wait()
        lax.fori_loop(first // 8, final // 8, step, 0, unroll=UNROLL)
        store = pltpu.make_async_copy(
            result.at[:, first:final, :], inner.at[:, first:final, :], store_sems.at[which]
        )
        store.start()
        stores.append(store)
    for block in lane_blocks(rows):
        values = [jnp.sum(sums[at, block, :].T, axis=0, keepdims=True) for at in range(6)]
        ends[:, block] = padded_rows(values, 8)
    for store in stores:
        store.wait()


def pack(values):
    return jnp.concatenate([values[0:6, block] for block in lane_blocks(values.shape[1])], axis=0)


def unpack(values):
    count = values.shape[0] // 6
    return jnp.concatenate([values[6 * at : 6 * at + 6, :] for at in range(count)], axis=1)


def write_shares(table, index, values, shares):
    swapped = pack(jnp.concatenate([values[3:6], values[0:3]], axis=0))
    values = pack(values)
    place = lax.broadcasted_iota(jnp.int32, values.shape, 0)
    third = jnp.zeros(values.shape, jnp.bool_)
    for at in range(0, values.shape[0], 6):
        third = third | ((place >= at) & (place < at + 3))
    for other in range(shares.shape[0]):
        base = 4 * other
        straight = jnp.where(third, table[index[0], base], table[index[0], base + 3])
        crossed = jnp.where(third, table[index[0], base + 1], table[index[0], base + 2])
        shares[other] = straight * values + crossed * swapped


def edge_lines(shape):
    rows = lax.broadcasted_iota(jnp.int32, shape, 0)
    line = rows - 3 * ((rows >= 3).astype(jnp.int32) + (rows >= 6).astype(jnp.int32))
    return rows, jnp.where(rows < 9, line, 3)


def halo_sides(before, after, curves, bends_head, bends_tail):
    _, line = edge_lines(before.shape)
    head = tail = None
    for k in (1, 2, 3):
        a, b = FIRST[k - 1], SECOND[k - 1]
        low = jnp.where(line < k, b * curves[0] - a * bends_head, 0.0)
        high = jnp.where((line >= 3 - k) & (line < 3), b * curves[1] + a * bends_tail, 0.0)
        low = low * (pltpu.roll(before, 16 - (3 - k), 0) if k < 3 else before)
        high = high * (pltpu.roll(after, 3 - k, 0) if k < 3 else after)
        head = low if head is None else head + low
        tail = high if tail is None else tail + high
    return head, tail


def tiled_lines(lines):
    return jnp.concatenate([lines, lines, lines, jnp.zeros((7, lines.shape[1]), F32)], axis=0)


def halo_kernel(
    scale, index, table, before_x, after_x, before_y, after_y, x_head, x_tail, y_head, y_tail,
    m1, m2, ends_y, near_ends, ends, shares, delta_x, delta_y,
):
    cells_x = before_y.shape[1]
    cells_y = before_x.shape[1]
    visc = scale * VISCOSITY
    head_x, tail_x = halo_sides(
        before_x[...],
        after_x[...],
        (visc, visc),
        -scale * tiled_lines(x_head[0:3, :]),
        -scale * tiled_lines(x_tail[0:3, :]),
    )
    first, last = slice(0, 128), slice(cells_y - 128, cells_y)
    near = padded_rows([m1[:, first], m1[:, last], m2[:, first], m2[:, last]], 128).T
    spread = [
        tiled_lines(jnp.broadcast_to(near[lines, at : at + 1], (3, cells_x)))
        for at, lines in enumerate((slice(0, 3), slice(125, 128), slice(0, 3), slice(125, 128)))
    ]
    slopes = spread[0:2]
    offsets = [visc * offset for offset in spread[2:4]]
    bends = [
        offsets[side] - (scale * slopes[side]) * tiled_lines(lines[3:6, :])
        for side, lines in enumerate((y_head, y_tail))
    ]
    head_y, tail_y = halo_sides(
        jnp.where(index[0] > 0, before_y[...], 0.0),
        jnp.where(index[0] < shares.shape[0] - 1, after_y[...], 0.0),
        [visc * slope * slope for slope in slopes],
        bends[0],
        bends[1],
    )
    delta_x[0:16, :] = head_x
    delta_x[16:32, :] = tail_x
    delta_y[0:16, :] = head_y
    delta_y[16:32, :] = tail_y
    values = ends[...] + lax.dot_general(
        near_ends[...],
        jnp.concatenate([head_y, tail_y], axis=0),
        (((1,), (0,)), ((), ())),
        precision=lax.Precision.HIGHEST,
        preferred_element_type=F32,
    )
    rows, line = edge_lines((16, 128))
    lane = lax.broadcasted_iota(jnp.int32, (16, 128), 1)
    extra = []
    for end in (0, 1):
        weights = ends_y[end : end + 1, :]
        first = jnp.sum(head_x * weights, axis=1, keepdims=True) * jnp.where(lane == line, 1.0, 0.0)
        final = jnp.sum(tail_x * weights, axis=1, keepdims=True) * jnp.where(lane == line + 125, 1.0, 0.0)
        for comp in range(3):
            own = (rows >= 3 * comp) & (rows < 3 * comp + 3)
            extra.append(
                jnp.concatenate(
                    [
                        jnp.sum(jnp.where(own, first, 0.0), axis=0, keepdims=True),
                        jnp.zeros((1, cells_x - 256), F32),
                        jnp.sum(jnp.where(own, final, 0.0), axis=0, keepdims=True),
                    ],
                    axis=1,
                )
            )
    write_shares(table, index, values + padded_rows(extra, 8), shares)


def turned_rows(rows, turned):
    tall = jnp.concatenate([rows, jnp.zeros((128 - rows.shape[0], rows.shape[1]), F32)], axis=0)
    for block in lane_blocks(rows.shape[1]):
        turned[block, :] = tall[:, block].T


def solve_kernel(
    inner, delta_x, delta_y, table_y, table_x, solved, edges,
    work, inverse_y, inverse_x, high, low, turned, sems,
):
    cells_x, cells = solved.shape[1], solved.shape[2]
    loads = [pltpu.make_async_copy(inner.at[comp], work.at[comp], sems.at[comp]) for comp in range(3)]
    tables_y = [pltpu.make_async_copy(table_y.at[at], inverse_y.at[at], sems.at[3 + at]) for at in (0, 1)]
    tables_x = [pltpu.make_async_copy(table_x.at[at], inverse_x.at[at], sems.at[5 + at]) for at in (0, 1)]
    for copy in loads[:1] + tables_y + tables_x + loads[1:]:
        copy.start()
    turned_rows(delta_y[...], turned)
    lane = lax.broadcasted_iota(jnp.int32, (128, 128), 1)
    half = cells_x // 2
    halves = (slice(0, half), slice(half, cells_x))
    for comp in range(3):
        loads[comp].wait()
        for block in lane_blocks(cells_x):
            tile = turned[block, :]
            near = pltpu.roll(tile, 128 - 3 * comp, 1) if comp else tile
            work[comp, block, 0:128] += jnp.where(lane < 3, near, 0.0)
            far = pltpu.roll(tile, 109 - 3 * comp, 1)
            work[comp, block, cells - 128 : cells] += jnp.where(lane >= 125, far, 0.0)
        work[comp, 0:3, :] += delta_x[3 * comp : 3 * comp + 3, :]
        work[comp, cells_x - 3 : cells_x, :] += delta_x[16 + 3 * comp : 19 + 3 * comp, :]
        if comp == 0:
            for copy in tables_y:
                copy.wait()
        for rows in halves:
            above, below = split(work[comp, rows, :])
            high[rows, :], low[rows, :] = split(
                jnp.dot(above, inverse_y[0], preferred_element_type=F32)
                + jnp.dot(below, inverse_y[0], preferred_element_type=F32)
                + jnp.dot(above, inverse_y[1], preferred_element_type=F32)
            )
        if comp == 0:
            for copy in tables_x:
                copy.wait()
        for rows in halves:
            solved[comp, rows, :] = (
                jnp.dot(inverse_x[0, rows, :], high[...], preferred_element_type=F32)
                + jnp.dot(inverse_x[0, rows, :], low[...], preferred_element_type=F32)
                + jnp.dot(inverse_x[1, rows, :], high[...], preferred_element_type=F32)
            )
    edges[...] = padded_rows(
        [solved[comp, 0:1, :] for comp in range(3)] + [solved[comp, cells_x - 1 : cells_x, :] for comp in range(3)], 8
    )


def chain_numbers(head, tail):
    gain = 1.0 / (1.0 - tail[-1] * head[0])
    return float(gain), float(gain * head[-1]), float(tail[-1]), float(head[0])


def ends_kernel(chain, got, edges, ends_x, sides_y, out, beside):
    gain, ratio, behind, _ = chain
    total = got[0]
    for block in range(1, got.shape[0]):
        total = total + got[block]
    total = unpack(total)
    beside[...] = padded_rows([total], 8)
    rows = []
    for end in (0, 1):
        value = jnp.sum(total * ends_x[end : end + 1, :], axis=1, keepdims=True)
        for comp in range(3):
            rows.append(
                value[comp : comp + 1] * sides_y[0:1, :] + value[comp + 3 : comp + 4] * sides_y[1:2, :]
            )
    values = edges[...] + padded_rows(rows, 8)
    links = gain * values[3:6] + (gain * ratio * behind) * values[0:3]
    out[...] = padded_rows([links, values[0:3]], 8)


def pair_kernel(chain, index, own, other, out):
    even = index[0] % 2 == 0
    first = jnp.where(even, own[...], other[...])
    second = jnp.where(even, other[...], own[...])
    out[...] = padded_rows([second[0:3] + chain[1] * first[0:3], first[3:6]], 8)


def window_kernel(chain, own, below, above, out):
    step = chain[1] * chain[1]
    out[...] = above[...] + step * own[...] + (step * step) * below[...]


def beside_kernel(solved, beside, sides_y, table, token, updated, inverse, turned, sems):
    cells_x, cells_y = solved.shape[1], solved.shape[2]
    copies = [pltpu.make_async_copy(table.at[at], inverse.at[at], sems.at[at]) for at in (0, 1)]
    for copy in copies:
        copy.start()
    high, low = split(padded_rows([beside[...]], 16))
    for copy in copies:
        copy.wait()
    turned_rows(
        jnp.dot(high, inverse[0], preferred_element_type=F32)
        + jnp.dot(low, inverse[0], preferred_element_type=F32)
        + jnp.dot(high, inverse[1], preferred_element_type=F32),
        turned,
    )
    before = jnp.broadcast_to(sides_y[0:1, :], (8, cells_y))
    after = jnp.broadcast_to(sides_y[1:2, :], (8, cells_y))

    def step(index, carry):
        rows = pl.ds(pl.multiple_of(index * 8, 8), 8)
        here = turned[rows, :]
        for comp in range(3):
            updated[comp, rows, :] = solved[comp, rows, :] + (
                here[:, comp : comp + 1] * before + here[:, comp + 3 : comp + 4] * after
            )
        return carry

    lax.fori_loop(0, cells_x // 8, step, 0, unroll=4)


def final_kernel(
    chain, chips, index, own, other, pair, pair_above, far_below, far_above, rows_x, solved,
    out, beyond, turned,
):
    step = pl.program_id(0)
    rows = out.shape[1]
    blocks = lane_blocks(out.shape[2])
    gain, ratio, behind, ahead = chain
    link = ratio * ratio

    @pl.when(step == 0)
    def _():
        turned_rows(rows_x[...], turned)
        even = index[0] % 2 == 0
        chip = (
            far_below[0:3, :]
            + link**3 * far_above[0:3, :]
            + (link**6 * pair_above[0:3, :] + link**7 * pair[0:3, :])
        ) * (1.0 / (1.0 - link**chips))
        before = jnp.where(even, chip, other[0:3, :] + ratio * chip)
        following = jnp.where(even, other[3:6, :], pair_above[3:6, :])
        first = (gain * behind) * own[3:6, :] + before
        last = gain * following + ahead * (own[0:3, :] + ratio * before)
        for comp in range(3):
            for side, values in enumerate((first, last)):
                wide = jnp.broadcast_to(values[comp : comp + 1, :], (8, values.shape[1]))
                for at, block in enumerate(blocks):
                    beyond[3 * side + comp, at] = wide[:, block]

    for at in range(0, rows, 8):
        where = pl.ds(pl.multiple_of(step * rows + at, 8), 8)
        here = turned[where, :]
        head = jnp.broadcast_to(here[:, 2:3], (8, 128))
        tail = jnp.broadcast_to(here[:, 3:4], (8, 128))
        for comp in range(3):
            for place, block in enumerate(blocks):
                out[comp, at : at + 8, block] = solved[comp, where, block] + (
                    head * beyond[comp, place] + tail * beyond[comp + 3, place]
                )


VMEM = pl.BlockSpec(memory_space=pltpu.VMEM)
SMEM = pl.BlockSpec(memory_space=pltpu.SMEM)
HBM = pl.BlockSpec(memory_space=pltpu.HBM)


def in_hbm(values):
    return pltpu.with_memory_space_constraint(values, pltpu.HBM)


def struct(*shape):
    return jax.ShapeDtypeStruct(shape, F32)


def call(kernel, in_specs, out_shape, scratch, flops, nbytes, **kinds):
    if "out_specs" not in kinds:
        kinds["out_specs"] = [VMEM] * len(out_shape)
    return pl.pallas_call(
        kernel,
        in_specs=in_specs,
        out_shape=out_shape,
        scratch_shapes=scratch,
        compiler_params=pltpu.CompilerParams(vmem_limit_bytes=VMEM_LIMIT),
        cost_estimate=pl.CostEstimate(flops=flops, bytes_accessed=nbytes, transcendentals=0),
        **kinds,
    )


def local(velocity, metric_first, metric_second):
    _, nx, ny = velocity.shape
    blocks_x, blocks_y = lax.axis_size("gx"), lax.axis_size("gy")
    low_x, up_x, diag_x, sig_x = coefficients(blocks_x * nx)
    low_y, up_y, diag_y, sig_y = coefficients(blocks_y * ny)
    scale = math.sqrt(sig_x * sig_y) / (diag_x * diag_y)
    inverse_x, head_x, tail_x, _ = line_tables(nx, low_x, up_x, blocks_x, True)
    inverse_y, head_y, tail_y, among_y = line_tables(ny, low_y, up_y, blocks_y, False)
    table_y = jnp.asarray(among_y.transpose(1, 0, 2, 3).reshape(blocks_y, 4 * blocks_y), F32)
    ends_x = jnp.asarray(np.stack([inverse_x[0], inverse_x[-1]]), F32)
    ends_y = jnp.asarray(np.stack([inverse_y[0], inverse_y[-1]]), F32)
    near = np.zeros((8, 32))
    for end, row in enumerate((inverse_y[0], inverse_y[-1])):
        for comp in range(3):
            near[3 * end + comp, 3 * comp : 3 * comp + 3] = row[:3]
            near[3 * end + comp, 16 + 3 * comp : 19 + 3 * comp] = row[-3:]
    near_ends = jnp.asarray(near, F32)
    rows_x = np.zeros((8, nx))
    rows_x[:4] = np.stack([inverse_x[0], inverse_x[-1], head_x, tail_x])
    rows_x = jnp.asarray(rows_x, F32)
    sides_y = jnp.asarray(np.stack([head_y, tail_y]), F32)
    parts_x = in_hbm(jnp.asarray(split_table(inverse_x)))
    turned_x = in_hbm(jnp.asarray(split_table(inverse_x.T)))
    parts_y = in_hbm(jnp.asarray(split_table(inverse_y.T)))
    index_x = lax.axis_index("gx").astype(jnp.int32).reshape(1)
    index_y = lax.axis_index("gy").astype(jnp.int32).reshape(1)
    m1 = metric_first.reshape(1, ny)
    m2 = metric_second.reshape(1, ny)
    cells = 3 * nx * ny
    round_x = [(i, (i + 1) % blocks_x) for i in range(blocks_x)]
    back_x = [(b, a) for a, b in round_x]
    round_y = [(i, (i + 1) % blocks_y) for i in range(blocks_y)]
    back_y = [(b, a) for a, b in round_y]

    velocity = in_hbm(velocity)
    with jax.named_scope("edges"):
        x_head, x_tail, y_head, y_tail = call(
            edges_kernel,
            [HBM],
            [struct(16, ny)] * 2 + [struct(16, nx)] * 2,
            [pltpu.VMEM((3, 8, ny), F32)] * 2
            + [pltpu.VMEM((3, nx, 128), F32)] * 2
            + [pltpu.SemaphoreType.DMA((2 + nx // 64,))],
            10 * nx * 128,
            24 * nx * 128,
        )(velocity)
    with jax.named_scope("halos"):
        before_x = lax.ppermute(x_tail, "gx", round_x)
        after_x = lax.ppermute(x_head, "gx", back_x)
        before_y = lax.ppermute(y_tail, "gy", round_y)
        after_y = lax.ppermute(y_head, "gy", back_y)
    with jax.named_scope("inner"):
        inner, ends = call(
            functools.partial(inner_kernel, scale),
            [HBM] + [VMEM] * 3,
            [pltpu.HBM((3, nx, ny), F32), struct(8, nx)],
            [
                pltpu.VMEM((3, ny // 128, nx + 16, 128), F32),
                pltpu.VMEM((3, nx, ny), F32),
                pltpu.VMEM((8, ny // 128, 8, 128), F32),
                pltpu.VMEM((6, nx, 128), F32),
                pltpu.SemaphoreType.DMA((len(CUTS) - 1, ny // 128)),
                pltpu.SemaphoreType.DMA((len(CUTS) - 1,)),
            ],
            40 * cells,
            8 * cells,
            out_specs=[HBM, VMEM],
        )(velocity, m1, m2, ends_y)
    with jax.named_scope("halo_part"):
        shares_y, delta_x, delta_y = call(
            functools.partial(halo_kernel, scale),
            [SMEM, SMEM] + [VMEM] * 13,
            [struct(blocks_y, 6 * (nx // 128), 128), struct(32, ny), struct(32, nx)],
            [],
            1000 * nx,
            500 * nx,
        )(
            index_y, table_y, before_x, after_x, before_y, after_y, x_head, x_tail, y_head, y_tail,
            m1, m2, ends_y, near_ends, ends,
        )
    with jax.named_scope("across_y"):
        got_y = lax.all_to_all(shares_y, "gy", 0, 0, tiled=True)
    with jax.named_scope("solve"):
        solved, edges = call(
            solve_kernel,
            [HBM] + [VMEM] * 2 + [HBM] * 2,
            [struct(3, nx, ny), struct(8, ny)],
            [pltpu.VMEM((3, nx, ny), F32), pltpu.VMEM((2, ny, ny), BF16), pltpu.VMEM((2, nx, nx), BF16)]
            + [pltpu.VMEM((nx, ny), BF16)] * 2
            + [pltpu.VMEM((nx, 128), F32), pltpu.SemaphoreType.DMA((7,))],
            6 * cells * (nx + ny),
            8 * cells,
        )(in_hbm(inner), delta_x, delta_y, parts_y, parts_x)
    chain = chain_numbers(head_x, tail_x)
    link = struct(8, ny)
    with jax.named_scope("ends_x"):
        own, beside = call(
            functools.partial(ends_kernel, chain),
            [VMEM] * 4,
            [link, struct(8, nx)],
            [],
            100 * nx,
            500 * nx,
        )(got_y, edges, ends_x, sides_y)

    def along(values, shift):
        return lax.ppermute(values, "gx", [(i, (i + shift) % blocks_x) for i in range(blocks_x)])

    with jax.named_scope("across_x"):
        other = lax.ppermute(own, "gx", [(i, i ^ 1) for i in range(blocks_x)])
        (pair,) = call(
            functools.partial(pair_kernel, chain), [SMEM, VMEM, VMEM], [link], [], 10 * nx, 100 * nx
        )(index_x, own, other)
        pair_below = along(pair, 2)
        pair_above = along(pair, -2)
        (window,) = call(functools.partial(window_kernel, chain), [VMEM] * 3, [link], [], 10 * nx, 100 * nx)(
            pair, pair_below, pair_above
        )
        far_below = along(window, 4)
        far_above = along(window, -6)
        (solved,) = call(
            beside_kernel,
            [VMEM] * 3 + [HBM, VMEM],
            [struct(3, nx, ny)],
            [pltpu.VMEM((2, nx, nx), BF16), pltpu.VMEM((nx, 128), F32), pltpu.SemaphoreType.DMA((2,))],
            6 * cells,
            8 * cells,
            input_output_aliases={0: 0},
        )(solved, beside, sides_y, turned_x, window)
    with jax.named_scope("final"):
        return call(
            functools.partial(final_kernel, chain, blocks_x // 2),
            [SMEM] + [VMEM] * 8,
            struct(3, nx, ny),
            [pltpu.VMEM((6, ny // 128, 8, 128), F32), pltpu.VMEM((nx, 128), F32)],
            4 * cells,
            8 * cells,
            grid=(nx // 128,),
            out_specs=pl.BlockSpec((3, 128, ny), lambda i: (0, i, 0)),
        )(index_x, own, other, pair, pair_above, far_below, far_above, rows_x, solved)


def solution(mesh):
    in_specs = (P(None, "gx", "gy"), P("gy"), P("gy"))
    out_specs = P(None, "gx", "gy")
    return jax.shard_map(local, mesh=mesh, in_specs=in_specs, out_specs=out_specs, check_vma=False)
```

```python
import functools
import math

import jax
import jax.numpy as jnp
import numpy as np
from jax import lax
from jax.experimental import pallas as pl
from jax.experimental.pallas import tpu as pltpu
from jax.sharding import PartitionSpec as P

VISCOSITY = 0.2
DIFFUSION = 1.0
FIRST = (45.0 / 60.0, -9.0 / 60.0, 1.0 / 60.0)
SECOND = (270.0 / 180.0, -27.0 / 180.0, 2.0 / 180.0)
CENTRE = -490.0 / 180.0
CUTS = (0, 4, 16, 64)
UNROLL = 16
OUT_CUTS = (0, 4, 16, 32, 48, 64)
F32 = jnp.float32
BF16 = jnp.bfloat16
VMEM_LIMIT = 24 * 1024 * 1024


def coefficients(cells):
    sigma = cells / 4.0
    diag = 1.0 + 2.0 * DIFFUSION + sigma
    return (-(DIFFUSION + sigma) / diag, -DIFFUSION / diag, diag, sigma)


def line_tables(length, lower, upper, blocks, periodic):
    matrix = np.eye(length) + lower * np.eye(length, k=-1) + upper * np.eye(length, k=1)
    inverse = np.linalg.inv(matrix)
    head = -lower * inverse[:, 0]
    tail = -upper * inverse[:, -1]
    order = 2 * blocks
    before = np.zeros((blocks, order))
    after = np.zeros((blocks, order))
    for block in range(blocks):
        if periodic or block > 0:
            before[block, 2 * ((block - 1) % blocks) + 1] = 1.0
        if periodic or block < blocks - 1:
            after[block, 2 * ((block + 1) % blocks)] = 1.0
    system = np.eye(order)
    for block in range(blocks):
        system[2 * block] -= head[0] * before[block] + tail[0] * after[block]
        system[2 * block + 1] -= head[-1] * before[block] + tail[-1] * after[block]
    solved = np.linalg.inv(system)
    sides = np.stack([before @ solved, after @ solved], axis=1)
    sides = sides.reshape(blocks, 2, blocks, 2).transpose(0, 2, 1, 3)
    return inverse, head, tail, sides


def split(values):
    high = values.astype(BF16)
    return high, (values - high.astype(F32)).astype(BF16)


def split_table(table):
    high = np.asarray(table, np.float32).astype(BF16)
    low = (np.asarray(table, np.float64) - high.astype(np.float64)).astype(BF16)
    return np.stack([high, low])


def padded_rows(rows, count):
    filled = sum(row.shape[0] for row in rows)
    return jnp.concatenate(rows + [jnp.zeros((count - filled, rows[0].shape[1]), F32)], axis=0)


def lane_blocks(cells):
    return [slice(at, at + 128) for at in range(0, cells, 128)]


def edges_kernel(field, x_head, x_tail, y_head, y_tail, top, bottom, left, right, sems):
    rows, cells = field.shape[1], field.shape[2]
    ends = [
        pltpu.make_async_copy(field.at[:, 0:8, :], top, sems.at[0]),
        pltpu.make_async_copy(field.at[:, rows - 8 : rows, :], bottom, sems.at[1]),
    ]
    blocks = lane_blocks(rows)
    sides = [
        [
            pltpu.make_async_copy(field.at[:, block, 0:128], left.at[:, block, :], sems.at[2 + 2 * at]),
            pltpu.make_async_copy(field.at[:, block, cells - 128 : cells], right.at[:, block, :], sems.at[3 + 2 * at]),
        ]
        for at, block in enumerate(blocks)
    ]
    for group in sides + [ends]:
        for copy in group:
            copy.start()
    x_head[9:16, :] = jnp.zeros((7, cells), F32)
    x_tail[9:16, :] = jnp.zeros((7, cells), F32)
    lane = lax.broadcasted_iota(jnp.int32, (128, 128), 1)
    for group, block in zip(sides, blocks):
        for copy in group:
            copy.wait()
        packed = left[0, block, :]
        for comp in range(3):
            if comp:
                packed = jnp.where(lane < 3 * comp, packed, pltpu.roll(left[comp, block, :], 3 * comp, 1))
        packed = jnp.where(lane < 9, packed, 0.0)
        for comp in range(3):
            here = pltpu.roll(right[comp, block, :], 19 + 3 * comp, 1)
            packed = jnp.where((lane >= 16 + 3 * comp) & (lane < 19 + 3 * comp), here, packed)
        turned = packed.T
        y_head[:, block] = turned[0:16, :]
        y_tail[:, block] = turned[16:32, :]
    for copy in ends:
        copy.wait()
    for comp in range(3):
        x_head[3 * comp : 3 * comp + 3, :] = top[comp, 0:3, :]
        x_tail[3 * comp : 3 * comp + 3, :] = bottom[comp, 5:8, :]


def inner_kernel(scale, field, m1, m2, ends_y, result, ends, padded, along_rows, sums, load_sems):
    rows, cells = result.shape[1], result.shape[2]
    blocks = lane_blocks(cells)
    count = len(blocks)
    visc = scale * VISCOSITY
    zero = jnp.zeros((8, 128), F32)
    bounds = [rows * at // 64 for at in CUTS]
    spans = list(zip(bounds[:-1], bounds[1:]))
    loads = []
    for which, (first, final) in enumerate(spans):
        low, high = (first + 8 if first else 0), min(final + 8, rows)
        loads.append(
            [
                pltpu.make_async_copy(
                    field.at[:, low:high, block], padded.at[:, at, low + 8 : high + 8, :], load_sems.at[which, at]
                )
                for at, block in enumerate(blocks)
            ]
        )
    for group in loads:
        for copy in group:
            copy.start()
    for comp in range(3):
        for at in range(count):
            padded[comp, at, 0:8, :] = zero
            padded[comp, at, 8 + rows : 16 + rows, :] = zero
    slope = m1[...]
    curve = visc * slope * slope
    for at, row in enumerate(
        [scale * slope, visc * m2[...], SECOND[0] * curve, SECOND[1] * curve, SECOND[2] * curve]
        + [CENTRE * (curve + visc), ends_y[0:1, :], ends_y[1:2, :]]
    ):
        wide = jnp.broadcast_to(row, (8, cells))
        for place, block in enumerate(blocks):
            along_rows[at, place] = wide[:, block]
    lane = lax.broadcasted_iota(jnp.int32, (8, 128), 1)

    def step(index, carry):
        row = pl.multiple_of(index * 8, 8)
        fields = [[padded[comp, at, pl.ds(row + 8, 8), :] for at in range(count)] for comp in range(3)]
        along = [scale * part for part in fields[0]]
        bend = [along_rows[1, at] - fields[1][at] * along_rows[0, at] for at in range(count)]
        totals = [[along_rows[5, at] * fields[comp][at] for at in range(count)] for comp in range(3)]
        for k in (1, 2, 3):
            lead = [FIRST[k - 1] * part for part in along]
            lean = [FIRST[k - 1] * part for part in bend]
            x_ahead = [visc * SECOND[k - 1] - part for part in lead]
            x_behind = [visc * SECOND[k - 1] + part for part in lead]
            y_ahead = [along_rows[1 + k, at] + lean[at] for at in range(count)]
            y_behind = [along_rows[1 + k, at] - lean[at] for at in range(count)]
            for comp in range(3):
                left = [pltpu.roll(part, 128 - k, 1) for part in fields[comp]] + [zero]
                right = [zero] + [pltpu.roll(part, k, 1) for part in fields[comp]]
                for at in range(count):
                    totals[comp][at] = (
                        totals[comp][at]
                        + (
                            x_ahead[at] * padded[comp, at, pl.ds(row + 8 + k, 8), :]
                            + x_behind[at] * padded[comp, at, pl.ds(row + 8 - k, 8), :]
                        )
                        + (
                            y_ahead[at] * jnp.where(lane < 128 - k, left[at], left[at + 1])
                            + y_behind[at] * jnp.where(lane >= k, right[at + 1], right[at])
                        )
                    )
        for comp in range(3):
            for end in (0, 1):
                value = totals[comp][0] * along_rows[6 + end, 0]
                for at in range(1, count):
                    value = value + totals[comp][at] * along_rows[6 + end, at]
                sums[3 * end + comp, pl.ds(row, 8), :] = value
            for at, block in enumerate(blocks):
                result[comp, pl.ds(row, 8), block] = totals[comp][at]
        return carry

    for which, (first, final) in enumerate(spans):
        for copy in loads[which]:
            copy.wait()
        lax.fori_loop(first // 8, final // 8, step, 0, unroll=min(UNROLL, (final - first) // 8))
    for block in lane_blocks(rows):
        values = [jnp.sum(sums[at, block, :].T, axis=0, keepdims=True) for at in range(6)]
        ends[:, block] = padded_rows(values, 8)


def pack(values):
    return jnp.concatenate([values[0:6, block] for block in lane_blocks(values.shape[1])], axis=0)


def unpack(values):
    count = values.shape[0] // 6
    return jnp.concatenate([values[6 * at : 6 * at + 6, :] for at in range(count)], axis=1)


def write_shares(table, index, values, shares):
    swapped = pack(jnp.concatenate([values[3:6], values[0:3]], axis=0))
    values = pack(values)
    place = lax.broadcasted_iota(jnp.int32, values.shape, 0)
    third = jnp.zeros(values.shape, jnp.bool_)
    for at in range(0, values.shape[0], 6):
        third = third | ((place >= at) & (place < at + 3))
    for other in range(shares.shape[0]):
        base = 4 * other
        straight = jnp.where(third, table[index[0], base], table[index[0], base + 3])
        crossed = jnp.where(third, table[index[0], base + 1], table[index[0], base + 2])
        shares[other] = straight * values + crossed * swapped


def edge_lines(shape):
    rows = lax.broadcasted_iota(jnp.int32, shape, 0)
    line = rows - 3 * ((rows >= 3).astype(jnp.int32) + (rows >= 6).astype(jnp.int32))
    return rows, jnp.where(rows < 9, line, 3)


def halo_sides(before, after, curves, bends_head, bends_tail):
    _, line = edge_lines(before.shape)
    head = tail = None
    for k in (1, 2, 3):
        a, b = FIRST[k - 1], SECOND[k - 1]
        low = jnp.where(line < k, b * curves[0] - a * bends_head, 0.0)
        high = jnp.where((line >= 3 - k) & (line < 3), b * curves[1] + a * bends_tail, 0.0)
        low = low * (pltpu.roll(before, 16 - (3 - k), 0) if k < 3 else before)
        high = high * (pltpu.roll(after, 3 - k, 0) if k < 3 else after)
        head = low if head is None else head + low
        tail = high if tail is None else tail + high
    return head, tail


def tiled_lines(lines):
    return jnp.concatenate([lines, lines, lines, jnp.zeros((7, lines.shape[1]), F32)], axis=0)


def halo_kernel(
    scale, index, table, before_x, after_x, before_y, after_y, x_head, x_tail, y_head, y_tail,
    m1, m2, ends_y, near_ends, ends, inner, shares, delta, kept, near_shares, near_delta, sems,
):
    cells_x = before_y.shape[1]
    cells_y = before_x.shape[1]
    visc = scale * VISCOSITY
    head_x, tail_x = halo_sides(
        before_x[...],
        after_x[...],
        (visc, visc),
        -scale * tiled_lines(x_head[0:3, :]),
        -scale * tiled_lines(x_tail[0:3, :]),
    )
    first, last = slice(0, 128), slice(cells_y - 128, cells_y)
    near = padded_rows([m1[:, first], m1[:, last], m2[:, first], m2[:, last]], 128).T
    spread = [
        tiled_lines(jnp.broadcast_to(near[lines, at : at + 1], (3, cells_x)))
        for at, lines in enumerate((slice(0, 3), slice(125, 128), slice(0, 3), slice(125, 128)))
    ]
    slopes = spread[0:2]
    offsets = [visc * offset for offset in spread[2:4]]
    bends = [
        offsets[side] - (scale * slopes[side]) * tiled_lines(lines[3:6, :])
        for side, lines in enumerate((y_head, y_tail))
    ]
    head_y, tail_y = halo_sides(
        jnp.where(index[0] > 0, before_y[...], 0.0),
        jnp.where(index[0] < shares.shape[0] - 1, after_y[...], 0.0),
        [visc * slope * slope for slope in slopes],
        bends[0],
        bends[1],
    )
    for at, part in enumerate((head_x, tail_x, head_y, tail_y)):
        near_delta[16 * at : 16 * at + 16, :] = part
    store = pltpu.make_async_copy(near_delta, delta, sems.at[0])
    store.start()
    values = ends[...] + lax.dot_general(
        near_ends[...],
        jnp.concatenate([head_y, tail_y], axis=0),
        (((1,), (0,)), ((), ())),
        precision=lax.Precision.HIGHEST,
        preferred_element_type=F32,
    )
    rows, line = edge_lines((16, 128))
    lane = lax.broadcasted_iota(jnp.int32, (16, 128), 1)
    extra = []
    for end in (0, 1):
        weights = ends_y[end : end + 1, :]
        first = jnp.sum(head_x * weights, axis=1, keepdims=True) * jnp.where(lane == line, 1.0, 0.0)
        final = jnp.sum(tail_x * weights, axis=1, keepdims=True) * jnp.where(lane == line + 125, 1.0, 0.0)
        for comp in range(3):
            own = (rows >= 3 * comp) & (rows < 3 * comp + 3)
            extra.append(
                jnp.concatenate(
                    [
                        jnp.sum(jnp.where(own, first, 0.0), axis=0, keepdims=True),
                        jnp.zeros((1, cells_x - 256), F32),
                        jnp.sum(jnp.where(own, final, 0.0), axis=0, keepdims=True),
                    ],
                    axis=1,
                )
            )
    write_shares(table, index, values + padded_rows(extra, 8), near_shares)
    leave = pltpu.make_async_copy(near_shares, shares, sems.at[1])
    leave.start()
    store.wait()
    leave.wait()


def turned_rows(rows, turned):
    tall = jnp.concatenate([rows, jnp.zeros((128 - rows.shape[0], rows.shape[1]), F32)], axis=0)
    for block in lane_blocks(rows.shape[1]):
        turned[block, :] = tall[:, block].T


def solve_kernel(
    inner, delta, table_y, table_x, solved, edges,
    near_delta, inverse_y, inverse_x, above, below, high, low, turned, sems,
):
    cells_x, cells = solved.shape[1], solved.shape[2]
    tables_y = [pltpu.make_async_copy(table_y.at[at], inverse_y.at[at], sems.at[at]) for at in (0, 1)]
    tables_x = [pltpu.make_async_copy(table_x.at[at], inverse_x.at[at], sems.at[2 + at]) for at in (0, 1)]
    sides = pltpu.make_async_copy(delta, near_delta, sems.at[4])
    for copy in [sides] + tables_y + tables_x:
        copy.start()
    sides.wait()
    turned_rows(near_delta[32:64, :], turned)
    lane = lax.broadcasted_iota(jnp.int32, (128, 128), 1)
    half = cells_x // 2
    halves = (slice(0, half), slice(half, cells_x))
    for comp in range(3):
        for block in lane_blocks(cells_x):
            tile = turned[block, :]
            near = pltpu.roll(tile, 128 - 3 * comp, 1) if comp else tile
            far = pltpu.roll(tile, 109 - 3 * comp, 1)
            full = jnp.concatenate(
                [
                    inner[comp, block, 0:128] + jnp.where(lane < 3, near, 0.0),
                    inner[comp, block, 128 : cells - 128],
                    inner[comp, block, cells - 128 : cells] + jnp.where(lane >= 125, far, 0.0),
                ],
                axis=1,
            )
            if block.start == 0:
                full = full + padded_rows([near_delta[3 * comp : 3 * comp + 3, :]], 128)
            if block.stop == cells_x:
                full = full + jnp.concatenate(
                    [jnp.zeros((125, cells), F32), near_delta[16 + 3 * comp : 19 + 3 * comp, :]], axis=0
                )
            above[block, :], below[block, :] = split(full)
        if comp == 0:
            for copy in tables_y:
                copy.wait()
        for rows in halves:
            high[rows, :], low[rows, :] = split(
                jnp.dot(above[rows, :], inverse_y[0], preferred_element_type=F32)
                + jnp.dot(below[rows, :], inverse_y[0], preferred_element_type=F32)
                + jnp.dot(above[rows, :], inverse_y[1], preferred_element_type=F32)
            )
        if comp == 0:
            for copy in tables_x:
                copy.wait()
        for rows in halves:
            solved[comp, rows, :] = (
                jnp.dot(inverse_x[0, rows, :], high[...], preferred_element_type=F32)
                + jnp.dot(inverse_x[0, rows, :], low[...], preferred_element_type=F32)
                + jnp.dot(inverse_x[1, rows, :], high[...], preferred_element_type=F32)
            )
    edges[...] = padded_rows(
        [solved[comp, 0:1, :] for comp in range(3)] + [solved[comp, cells_x - 1 : cells_x, :] for comp in range(3)], 8
    )


def chain_numbers(head, tail):
    gain = 1.0 / (1.0 - tail[-1] * head[0])
    return float(gain), float(gain * head[-1]), float(tail[-1]), float(head[0])


def ends_kernel(chain, got, edges, ends_x, sides_y, out, beside):
    gain, ratio, behind, _ = chain
    total = got[0]
    for block in range(1, got.shape[0]):
        total = total + got[block]
    total = unpack(total)
    beside[...] = padded_rows([total], 8)
    rows = []
    for end in (0, 1):
        value = jnp.sum(total * ends_x[end : end + 1, :], axis=1, keepdims=True)
        for comp in range(3):
            rows.append(
                value[comp : comp + 1] * sides_y[0:1, :] + value[comp + 3 : comp + 4] * sides_y[1:2, :]
            )
    values = edges[...] + padded_rows(rows, 8)
    links = gain * values[3:6] + (gain * ratio * behind) * values[0:3]
    out[...] = padded_rows([links, values[0:3]], 8)


def pair_kernel(chain, index, own, other, out):
    even = index[0] % 2 == 0
    first = jnp.where(even, own[...], other[...])
    second = jnp.where(even, other[...], own[...])
    out[...] = padded_rows([second[0:3] + chain[1] * first[0:3], first[3:6]], 8)


def window_kernel(chain, own, below, above, out):
    step = chain[1] * chain[1]
    out[...] = above[...] + step * own[...] + (step * step) * below[...]


def columns_kernel(beside, table, sides_x, token, turned, inverse, sems):
    copies = [pltpu.make_async_copy(table.at[at], inverse.at[at], sems.at[at]) for at in (0, 1)]
    for copy in copies:
        copy.start()
    high, low = split(padded_rows([beside[...]], 16))
    for copy in copies:
        copy.wait()
    lines = (
        jnp.dot(high, inverse[0], preferred_element_type=F32)
        + jnp.dot(low, inverse[0], preferred_element_type=F32)
        + jnp.dot(high, inverse[1], preferred_element_type=F32)
    )
    turned_rows(jnp.concatenate([lines[0:6], sides_x[...]], axis=0), turned)


def beside_kernel(solved, turned, sides_y, token, updated):
    cells_x, cells_y = solved.shape[1], solved.shape[2]
    before = jnp.broadcast_to(sides_y[0:1, :], (8, cells_y))
    after = jnp.broadcast_to(sides_y[1:2, :], (8, cells_y))

    def step(index, carry):
        rows = pl.ds(pl.multiple_of(index * 8, 8), 8)
        here = turned[rows, :]
        for comp in range(3):
            updated[comp, rows, :] = solved[comp, rows, :] + (
                here[:, comp : comp + 1] * before + here[:, comp + 3 : comp + 4] * after
            )
        return carry

    lax.fori_loop(0, cells_x // 8, step, 0, unroll=4)


def final_kernel(
    chain, chips, index, own, other, pair, pair_above, far_below, far_above, turned, solved,
    out, beyond, result, sems,
):
    rows = out.shape[1]
    blocks = lane_blocks(out.shape[2])
    gain, ratio, behind, ahead = chain
    link = ratio * ratio

    even = index[0] % 2 == 0
    chip = (
        far_below[0:3, :]
        + link**3 * far_above[0:3, :]
        + (link**6 * pair_above[0:3, :] + link**7 * pair[0:3, :])
    ) * (1.0 / (1.0 - link**chips))
    before = jnp.where(even, chip, other[0:3, :] + ratio * chip)
    following = jnp.where(even, other[3:6, :], pair_above[3:6, :])
    first = (gain * behind) * own[3:6, :] + before
    last = gain * following + ahead * (own[0:3, :] + ratio * before)
    for comp in range(3):
        for side, values in enumerate((first, last)):
            wide = jnp.broadcast_to(values[comp : comp + 1, :], (8, values.shape[1]))
            for at, block in enumerate(blocks):
                beyond[3 * side + comp, at] = wide[:, block]

    def step(index, carry):
        where = pl.ds(pl.multiple_of(index * 8, 8), 8)
        here = turned[where, :]
        head = jnp.broadcast_to(here[:, 6:7], (8, 128))
        tail = jnp.broadcast_to(here[:, 7:8], (8, 128))
        for comp in range(3):
            for place, block in enumerate(blocks):
                result[comp, where, block] = solved[comp, where, block] + (
                    head * beyond[comp, place] + tail * beyond[comp + 3, place]
                )
        return carry

    stores = []
    bounds = [rows * at // 64 for at in OUT_CUTS]
    for which, (low, high) in enumerate(zip(bounds[:-1], bounds[1:])):
        lax.fori_loop(low // 8, high // 8, step, 0, unroll=4)
        store = pltpu.make_async_copy(result.at[:, low:high, :], out.at[:, low:high, :], sems.at[which])
        store.start()
        stores.append(store)
    for store in stores:
        store.wait()


VMEM = pl.BlockSpec(memory_space=pltpu.VMEM)
SMEM = pl.BlockSpec(memory_space=pltpu.SMEM)
HBM = pl.BlockSpec(memory_space=pltpu.HBM)
ANY = pl.BlockSpec(memory_space=pl.ANY)


def in_hbm(values):
    return pltpu.with_memory_space_constraint(values, pltpu.HBM)


def struct(*shape):
    return jax.ShapeDtypeStruct(shape, F32)


def call(kernel, in_specs, out_shape, scratch, flops, nbytes, **kinds):
    if "out_specs" not in kinds:
        kinds["out_specs"] = [VMEM] * len(out_shape)
    return pl.pallas_call(
        kernel,
        in_specs=in_specs,
        out_shape=out_shape,
        scratch_shapes=scratch,
        compiler_params=pltpu.CompilerParams(vmem_limit_bytes=VMEM_LIMIT),
        cost_estimate=pl.CostEstimate(flops=flops, bytes_accessed=nbytes, transcendentals=0),
        **kinds,
    )


def local(velocity, metric_first, metric_second):
    _, nx, ny = velocity.shape
    blocks_x, blocks_y = lax.axis_size("gx"), lax.axis_size("gy")
    low_x, up_x, diag_x, sig_x = coefficients(blocks_x * nx)
    low_y, up_y, diag_y, sig_y = coefficients(blocks_y * ny)
    scale = math.sqrt(sig_x * sig_y) / (diag_x * diag_y)
    inverse_x, head_x, tail_x, _ = line_tables(nx, low_x, up_x, blocks_x, True)
    inverse_y, head_y, tail_y, among_y = line_tables(ny, low_y, up_y, blocks_y, False)
    table_y = jnp.asarray(among_y.transpose(1, 0, 2, 3).reshape(blocks_y, 4 * blocks_y), F32)
    ends_x = jnp.asarray(np.stack([inverse_x[0], inverse_x[-1]]), F32)
    ends_y = jnp.asarray(np.stack([inverse_y[0], inverse_y[-1]]), F32)
    near = np.zeros((8, 32))
    for end, row in enumerate((inverse_y[0], inverse_y[-1])):
        for comp in range(3):
            near[3 * end + comp, 3 * comp : 3 * comp + 3] = row[:3]
            near[3 * end + comp, 16 + 3 * comp : 19 + 3 * comp] = row[-3:]
    near_ends = jnp.asarray(near, F32)
    sides_x = jnp.asarray(np.stack([head_x, tail_x]), F32)
    sides_y = jnp.asarray(np.stack([head_y, tail_y]), F32)
    parts_x = in_hbm(jnp.asarray(split_table(inverse_x)))
    turned_x = in_hbm(jnp.asarray(split_table(inverse_x.T)))
    parts_y = in_hbm(jnp.asarray(split_table(inverse_y.T)))
    index_x = lax.axis_index("gx").astype(jnp.int32).reshape(1)
    index_y = lax.axis_index("gy").astype(jnp.int32).reshape(1)
    m1 = metric_first.reshape(1, ny)
    m2 = metric_second.reshape(1, ny)
    cells = 3 * nx * ny
    round_x = [(i, (i + 1) % blocks_x) for i in range(blocks_x)]
    back_x = [(b, a) for a, b in round_x]
    round_y = [(i, (i + 1) % blocks_y) for i in range(blocks_y)]
    back_y = [(b, a) for a, b in round_y]

    velocity = in_hbm(velocity)
    with jax.named_scope("edges"):
        x_head, x_tail, y_head, y_tail = call(
            edges_kernel,
            [HBM],
            [struct(16, ny)] * 2 + [struct(16, nx)] * 2,
            [pltpu.VMEM((3, 8, ny), F32)] * 2
            + [pltpu.VMEM((3, nx, 128), F32)] * 2
            + [pltpu.SemaphoreType.DMA((2 + nx // 64,))],
            10 * nx * 128,
            24 * nx * 128,
        )(velocity)
    with jax.named_scope("halos"):
        before_x = lax.ppermute(x_tail, "gx", round_x)
        after_x = lax.ppermute(x_head, "gx", back_x)
        before_y = lax.ppermute(y_tail, "gy", round_y)
        after_y = lax.ppermute(y_head, "gy", back_y)
    with jax.named_scope("inner"):
        inner, ends = call(
            functools.partial(inner_kernel, scale),
            [HBM] + [VMEM] * 3,
            [struct(3, nx, ny), struct(8, nx)],
            [
                pltpu.VMEM((3, ny // 128, nx + 16, 128), F32),
                pltpu.VMEM((8, ny // 128, 8, 128), F32),
                pltpu.VMEM((6, nx, 128), F32),
                pltpu.SemaphoreType.DMA((len(CUTS) - 1, ny // 128)),
            ],
            40 * cells,
            8 * cells,
        )(velocity, m1, m2, ends_y)
    with jax.named_scope("halo_part"):
        shares_y, delta, inner = call(
            functools.partial(halo_kernel, scale),
            [SMEM, SMEM] + [VMEM] * 13 + [ANY],
            [pltpu.HBM((blocks_y, 6 * (nx // 128), 128), F32), pltpu.HBM((64, ny), F32), struct(3, nx, ny)],
            [pltpu.VMEM((blocks_y, 6 * (nx // 128), 128), F32), pltpu.VMEM((64, ny), F32)]
            + [pltpu.SemaphoreType.DMA((2,))],
            1000 * nx,
            500 * nx,
            input_output_aliases={15: 2},
            out_specs=[HBM, HBM, ANY],
        )(
            index_y, table_y, before_x, after_x, before_y, after_y, x_head, x_tail, y_head, y_tail,
            m1, m2, ends_y, near_ends, ends, inner,
        )
    with jax.named_scope("across_y"):
        got_y = lax.all_to_all(shares_y, "gy", 0, 0, tiled=True)
    with jax.named_scope("solve"):
        solved, edges = call(
            solve_kernel,
            [VMEM] + [HBM] * 3,
            [struct(3, nx, ny), struct(8, ny)],
            [pltpu.VMEM((64, ny), F32), pltpu.VMEM((2, ny, ny), BF16), pltpu.VMEM((2, nx, nx), BF16)]
            + [pltpu.VMEM((nx, ny), BF16)] * 4
            + [pltpu.VMEM((nx, 128), F32), pltpu.SemaphoreType.DMA((5,))],
            6 * cells * (nx + ny),
            8 * cells,
            input_output_aliases={0: 0},
        )(inner, in_hbm(delta), parts_y, parts_x)
    chain = chain_numbers(head_x, tail_x)
    link = struct(8, ny)
    with jax.named_scope("ends_x"):
        own, beside = call(
            functools.partial(ends_kernel, chain),
            [VMEM] * 4,
            [link, struct(8, nx)],
            [],
            100 * nx,
            500 * nx,
        )(got_y, edges, ends_x, sides_y)

    def along(values, shift):
        return lax.ppermute(values, "gx", [(i, (i + shift) % blocks_x) for i in range(blocks_x)])

    with jax.named_scope("across_x"):
        other = lax.ppermute(own, "gx", [(i, i ^ 1) for i in range(blocks_x)])
        (pair,) = call(
            functools.partial(pair_kernel, chain), [SMEM, VMEM, VMEM], [link], [], 10 * nx, 100 * nx
        )(index_x, own, other)
        pair_below = along(pair, 2)
        pair_above = along(pair, -2)
        (turned,) = call(
            columns_kernel,
            [VMEM, HBM, VMEM, VMEM],
            [struct(nx, 128)],
            [pltpu.VMEM((2, nx, nx), BF16), pltpu.SemaphoreType.DMA((2,))],
            48 * nx * nx,
            4 * nx * nx,
        )(beside, turned_x, sides_x, pair)
        (window,) = call(functools.partial(window_kernel, chain), [VMEM] * 3, [link], [], 10 * nx, 100 * nx)(
            pair, pair_below, pair_above
        )
        far_below = along(window, 4)
        far_above = along(window, -6)
        (solved,) = call(
            beside_kernel,
            [VMEM] * 4,
            [struct(3, nx, ny)],
            [],
            6 * cells,
            8 * cells,
            input_output_aliases={0: 0},
        )(solved, turned, sides_y, window)
    with jax.named_scope("final"):
        return call(
            functools.partial(final_kernel, chain, blocks_x // 2),
            [SMEM] + [VMEM] * 8,
            struct(3, nx, ny),
            [pltpu.VMEM((6, ny // 128, 8, 128), F32), pltpu.VMEM((3, nx, ny), F32)]
            + [pltpu.SemaphoreType.DMA((len(OUT_CUTS) - 1,))],
            4 * cells,
            8 * cells,
            out_specs=ANY,
        )(index_x, own, other, pair, pair_above, far_below, far_above, turned, solved)


def solution(mesh):
    in_specs = (P(None, "gx", "gy"), P("gy"), P("gy"))
    out_specs = P(None, "gx", "gy")
    return jax.shard_map(local, mesh=mesh, in_specs=in_specs, out_specs=out_specs, check_vma=False)
```

```python
import functools
import math

import jax
import jax.numpy as jnp
import numpy as np
from jax import lax
from jax.experimental import pallas as pl
from jax.experimental.pallas import tpu as pltpu
from jax.sharding import PartitionSpec as P

VISCOSITY = 0.2
DIFFUSION = 1.0
FIRST = (45.0 / 60.0, -9.0 / 60.0, 1.0 / 60.0)
SECOND = (270.0 / 180.0, -27.0 / 180.0, 2.0 / 180.0)
CENTRE = -490.0 / 180.0
CUTS = (0, 4, 16, 64)
UNROLL = 16
LATER = 2
OUT_CUTS = (0, 4, 16, 32, 48, 64)
F32 = jnp.float32
BF16 = jnp.bfloat16
VMEM_LIMIT = 24 * 1024 * 1024


def coefficients(cells):
    sigma = cells / 4.0
    diag = 1.0 + 2.0 * DIFFUSION + sigma
    return (-(DIFFUSION + sigma) / diag, -DIFFUSION / diag, diag, sigma)


def line_tables(length, lower, upper, blocks, periodic):
    matrix = np.eye(length) + lower * np.eye(length, k=-1) + upper * np.eye(length, k=1)
    inverse = np.linalg.inv(matrix)
    head = -lower * inverse[:, 0]
    tail = -upper * inverse[:, -1]
    order = 2 * blocks
    before = np.zeros((blocks, order))
    after = np.zeros((blocks, order))
    for block in range(blocks):
        if periodic or block > 0:
            before[block, 2 * ((block - 1) % blocks) + 1] = 1.0
        if periodic or block < blocks - 1:
            after[block, 2 * ((block + 1) % blocks)] = 1.0
    system = np.eye(order)
    for block in range(blocks):
        system[2 * block] -= head[0] * before[block] + tail[0] * after[block]
        system[2 * block + 1] -= head[-1] * before[block] + tail[-1] * after[block]
    solved = np.linalg.inv(system)
    sides = np.stack([before @ solved, after @ solved], axis=1)
    sides = sides.reshape(blocks, 2, blocks, 2).transpose(0, 2, 1, 3)
    return inverse, head, tail, sides


def split(values):
    high = values.astype(BF16)
    return high, (values - high.astype(F32)).astype(BF16)


def split_table(table):
    high = np.asarray(table, np.float32).astype(BF16)
    low = (np.asarray(table, np.float64) - high.astype(np.float64)).astype(BF16)
    return np.stack([high, low])


def padded_rows(rows, count):
    filled = sum(row.shape[0] for row in rows)
    return jnp.concatenate(rows + [jnp.zeros((count - filled, rows[0].shape[1]), F32)], axis=0)


def lane_blocks(cells):
    return [slice(at, at + 128) for at in range(0, cells, 128)]


def edges_kernel(field, x_head, x_tail, y_head, y_tail, top, bottom, left, right, sems):
    rows, cells = field.shape[1], field.shape[2]
    ends = [
        pltpu.make_async_copy(field.at[:, 0:8, :], top, sems.at[0]),
        pltpu.make_async_copy(field.at[:, rows - 8 : rows, :], bottom, sems.at[1]),
    ]
    blocks = lane_blocks(rows)
    sides = [
        [
            pltpu.make_async_copy(field.at[:, block, 0:128], left.at[:, block, :], sems.at[2 + 2 * at]),
            pltpu.make_async_copy(field.at[:, block, cells - 128 : cells], right.at[:, block, :], sems.at[3 + 2 * at]),
        ]
        for at, block in enumerate(blocks)
    ]
    for group in sides + [ends]:
        for copy in group:
            copy.start()
    x_head[9:16, :] = jnp.zeros((7, cells), F32)
    x_tail[9:16, :] = jnp.zeros((7, cells), F32)
    lane = lax.broadcasted_iota(jnp.int32, (128, 128), 1)
    for group, block in zip(sides, blocks):
        for copy in group:
            copy.wait()
        packed = left[0, block, :]
        for comp in range(3):
            if comp:
                packed = jnp.where(lane < 3 * comp, packed, pltpu.roll(left[comp, block, :], 3 * comp, 1))
        packed = jnp.where(lane < 9, packed, 0.0)
        for comp in range(3):
            here = pltpu.roll(right[comp, block, :], 19 + 3 * comp, 1)
            packed = jnp.where((lane >= 16 + 3 * comp) & (lane < 19 + 3 * comp), here, packed)
        turned = packed.T
        y_head[:, block] = turned[0:16, :]
        y_tail[:, block] = turned[16:32, :]
    for copy in ends:
        copy.wait()
    for comp in range(3):
        x_head[3 * comp : 3 * comp + 3, :] = top[comp, 0:3, :]
        x_tail[3 * comp : 3 * comp + 3, :] = bottom[comp, 5:8, :]


def inner_kernel(scale, field, m1, m2, ends_y, result, ends, padded, along_rows, sums, load_sems):
    rows, cells = result.shape[1], result.shape[2]
    blocks = lane_blocks(cells)
    count = len(blocks)
    visc = scale * VISCOSITY
    zero = jnp.zeros((8, 128), F32)
    bounds = [rows * at // 64 for at in CUTS]
    spans = list(zip(bounds[:-1], bounds[1:]))
    loads = []
    for which, (first, final) in enumerate(spans):
        low, high = (first + 8 if first else 0), min(final + 8, rows)
        loads.append(
            [
                pltpu.make_async_copy(
                    field.at[:, low:high, block], padded.at[:, at, low + 8 : high + 8, :], load_sems.at[which, at]
                )
                for at, block in enumerate(blocks)
            ]
        )
    for group in loads:
        for copy in group:
            copy.start()
    for comp in range(3):
        for at in range(count):
            padded[comp, at, 0:8, :] = zero
            padded[comp, at, 8 + rows : 16 + rows, :] = zero
    slope = m1[...]
    curve = visc * slope * slope
    for at, row in enumerate(
        [scale * slope, visc * m2[...], SECOND[0] * curve, SECOND[1] * curve, SECOND[2] * curve]
        + [CENTRE * (curve + visc), ends_y[0:1, :], ends_y[1:2, :]]
    ):
        wide = jnp.broadcast_to(row, (8, cells))
        for place, block in enumerate(blocks):
            along_rows[at, place] = wide[:, block]
    lane = lax.broadcasted_iota(jnp.int32, (8, 128), 1)

    def step(index, carry):
        row = pl.multiple_of(index * 8, 8)
        fields = [[padded[comp, at, pl.ds(row + 8, 8), :] for at in range(count)] for comp in range(3)]
        along = [scale * part for part in fields[0]]
        bend = [along_rows[1, at] - fields[1][at] * along_rows[0, at] for at in range(count)]
        totals = [[along_rows[5, at] * fields[comp][at] for at in range(count)] for comp in range(3)]
        for k in (1, 2, 3):
            lead = [FIRST[k - 1] * part for part in along]
            lean = [FIRST[k - 1] * part for part in bend]
            x_ahead = [visc * SECOND[k - 1] - part for part in lead]
            x_behind = [visc * SECOND[k - 1] + part for part in lead]
            y_ahead = [along_rows[1 + k, at] + lean[at] for at in range(count)]
            y_behind = [along_rows[1 + k, at] - lean[at] for at in range(count)]
            for comp in range(3):
                left = [pltpu.roll(part, 128 - k, 1) for part in fields[comp]] + [zero]
                right = [zero] + [pltpu.roll(part, k, 1) for part in fields[comp]]
                for at in range(count):
                    totals[comp][at] = (
                        totals[comp][at]
                        + (
                            x_ahead[at] * padded[comp, at, pl.ds(row + 8 + k, 8), :]
                            + x_behind[at] * padded[comp, at, pl.ds(row + 8 - k, 8), :]
                        )
                        + (
                            y_ahead[at] * jnp.where(lane < 128 - k, left[at], left[at + 1])
                            + y_behind[at] * jnp.where(lane >= k, right[at + 1], right[at])
                        )
                    )
        for comp in range(3):
            for end in (0, 1):
                value = totals[comp][0] * along_rows[6 + end, 0]
                for at in range(1, count):
                    value = value + totals[comp][at] * along_rows[6 + end, at]
                sums[3 * end + comp, pl.ds(row, 8), :] = value
            for at, block in enumerate(blocks):
                result[comp, pl.ds(row, 8), block] = totals[comp][at]
        return carry

    for which, (first, final) in enumerate(spans):
        for copy in loads[which]:
            copy.wait()
        lax.fori_loop(first // 8, final // 8, step, 0, unroll=min(UNROLL, (final - first) // 8))
    for block in lane_blocks(rows):
        values = [jnp.sum(sums[at, block, :].T, axis=0, keepdims=True) for at in range(6)]
        ends[:, block] = padded_rows(values, 8)


def pack(values):
    return jnp.concatenate([values[0:6, block] for block in lane_blocks(values.shape[1])], axis=0)


def unpack(values):
    count = values.shape[0] // 6
    return jnp.concatenate([values[6 * at : 6 * at + 6, :] for at in range(count)], axis=1)


def write_shares(table, index, values, shares):
    swapped = pack(jnp.concatenate([values[3:6], values[0:3]], axis=0))
    values = pack(values)
    place = lax.broadcasted_iota(jnp.int32, values.shape, 0)
    third = jnp.zeros(values.shape, jnp.bool_)
    for at in range(0, values.shape[0], 6):
        third = third | ((place >= at) & (place < at + 3))
    for other in range(shares.shape[0]):
        base = 4 * other
        straight = jnp.where(third, table[index[0], base], table[index[0], base + 3])
        crossed = jnp.where(third, table[index[0], base + 1], table[index[0], base + 2])
        shares[other] = straight * values + crossed * swapped


def edge_lines(shape):
    rows = lax.broadcasted_iota(jnp.int32, shape, 0)
    line = rows - 3 * ((rows >= 3).astype(jnp.int32) + (rows >= 6).astype(jnp.int32))
    return rows, jnp.where(rows < 9, line, 3)


def halo_sides(before, after, curves, bends_head, bends_tail):
    _, line = edge_lines(before.shape)
    head = tail = None
    for k in (1, 2, 3):
        a, b = FIRST[k - 1], SECOND[k - 1]
        low = jnp.where(line < k, b * curves[0] - a * bends_head, 0.0)
        high = jnp.where((line >= 3 - k) & (line < 3), b * curves[1] + a * bends_tail, 0.0)
        low = low * (pltpu.roll(before, 16 - (3 - k), 0) if k < 3 else before)
        high = high * (pltpu.roll(after, 3 - k, 0) if k < 3 else after)
        head = low if head is None else head + low
        tail = high if tail is None else tail + high
    return head, tail


def tiled_lines(lines):
    return jnp.concatenate([lines, lines, lines, jnp.zeros((7, lines.shape[1]), F32)], axis=0)


def halo_kernel(
    scale, index, table, before_x, after_x, before_y, after_y, x_head, x_tail, y_head, y_tail,
    m1, m2, ends_y, near_ends, ends, inner, shares, delta, kept, near_shares, near_delta, sems,
):
    cells_x = before_y.shape[1]
    cells_y = before_x.shape[1]
    visc = scale * VISCOSITY
    head_x, tail_x = halo_sides(
        before_x[...],
        after_x[...],
        (visc, visc),
        -scale * tiled_lines(x_head[0:3, :]),
        -scale * tiled_lines(x_tail[0:3, :]),
    )
    first, last = slice(0, 128), slice(cells_y - 128, cells_y)
    near = padded_rows([m1[:, first], m1[:, last], m2[:, first], m2[:, last]], 128).T
    spread = [
        tiled_lines(jnp.broadcast_to(near[lines, at : at + 1], (3, cells_x)))
        for at, lines in enumerate((slice(0, 3), slice(125, 128), slice(0, 3), slice(125, 128)))
    ]
    slopes = spread[0:2]
    offsets = [visc * offset for offset in spread[2:4]]
    bends = [
        offsets[side] - (scale * slopes[side]) * tiled_lines(lines[3:6, :])
        for side, lines in enumerate((y_head, y_tail))
    ]
    head_y, tail_y = halo_sides(
        jnp.where(index[0] > 0, before_y[...], 0.0),
        jnp.where(index[0] < shares.shape[0] - 1, after_y[...], 0.0),
        [visc * slope * slope for slope in slopes],
        bends[0],
        bends[1],
    )
    for at, part in enumerate((head_x, tail_x, head_y, tail_y)):
        near_delta[16 * at : 16 * at + 16, :] = part
    store = pltpu.make_async_copy(near_delta, delta, sems.at[0])
    store.start()
    values = ends[...] + lax.dot_general(
        near_ends[...],
        jnp.concatenate([head_y, tail_y], axis=0),
        (((1,), (0,)), ((), ())),
        precision=lax.Precision.HIGHEST,
        preferred_element_type=F32,
    )
    rows, line = edge_lines((16, 128))
    lane = lax.broadcasted_iota(jnp.int32, (16, 128), 1)
    extra = []
    for end in (0, 1):
        weights = ends_y[end : end + 1, :]
        first = jnp.sum(head_x * weights, axis=1, keepdims=True) * jnp.where(lane == line, 1.0, 0.0)
        final = jnp.sum(tail_x * weights, axis=1, keepdims=True) * jnp.where(lane == line + 125, 1.0, 0.0)
        for comp in range(3):
            own = (rows >= 3 * comp) & (rows < 3 * comp + 3)
            extra.append(
                jnp.concatenate(
                    [
                        jnp.sum(jnp.where(own, first, 0.0), axis=0, keepdims=True),
                        jnp.zeros((1, cells_x - 256), F32),
                        jnp.sum(jnp.where(own, final, 0.0), axis=0, keepdims=True),
                    ],
                    axis=1,
                )
            )
    write_shares(table, index, values + padded_rows(extra, 8), near_shares)
    leave = pltpu.make_async_copy(near_shares, shares, sems.at[1])
    leave.start()
    store.wait()
    leave.wait()


def turned_rows(rows, turned):
    tall = jnp.concatenate([rows, jnp.zeros((128 - rows.shape[0], rows.shape[1]), F32)], axis=0)
    for block in lane_blocks(rows.shape[1]):
        turned[block, :] = tall[:, block].T


def solve_kernel(
    inner, delta, table_y, table_x, solved, edges,
    near_delta, inverse_y, inverse_x, above, below, high, low, turned, sems,
):
    cells_x, cells = solved.shape[1], solved.shape[2]
    tables_y = [pltpu.make_async_copy(table_y.at[at], inverse_y.at[at], sems.at[at]) for at in (0, 1)]
    tables_x = [pltpu.make_async_copy(table_x.at[at], inverse_x.at[at], sems.at[2 + at]) for at in (0, 1)]
    sides = pltpu.make_async_copy(delta, near_delta, sems.at[4])
    for copy in [sides] + tables_y + tables_x:
        copy.start()
    sides.wait()
    turned_rows(near_delta[32:64, :], turned)
    lane = lax.broadcasted_iota(jnp.int32, (128, 128), 1)
    half = cells_x // 2
    halves = (slice(0, half), slice(half, cells_x))
    for comp in range(3):
        for block in lane_blocks(cells_x):
            tile = turned[block, :]
            near = pltpu.roll(tile, 128 - 3 * comp, 1) if comp else tile
            far = pltpu.roll(tile, 109 - 3 * comp, 1)
            full = jnp.concatenate(
                [
                    inner[comp, block, 0:128] + jnp.where(lane < 3, near, 0.0),
                    inner[comp, block, 128 : cells - 128],
                    inner[comp, block, cells - 128 : cells] + jnp.where(lane >= 125, far, 0.0),
                ],
                axis=1,
            )
            if block.start == 0:
                full = full + padded_rows([near_delta[3 * comp : 3 * comp + 3, :]], 128)
            if block.stop == cells_x:
                full = full + jnp.concatenate(
                    [jnp.zeros((125, cells), F32), near_delta[16 + 3 * comp : 19 + 3 * comp, :]], axis=0
                )
            above[block, :], below[block, :] = split(full)
        if comp == 0:
            for copy in tables_y:
                copy.wait()
        for rows in halves:
            found = (
                jnp.dot(above[rows, :], inverse_y[0], preferred_element_type=F32)
                + jnp.dot(below[rows, :], inverse_y[0], preferred_element_type=F32)
                + jnp.dot(above[rows, :], inverse_y[1], preferred_element_type=F32)
            )
            high[rows, :], low[rows, :] = split(found)
            if comp == LATER:
                solved[comp, rows, :] = found
        if comp == 0:
            for copy in tables_x:
                copy.wait()
        if comp == LATER:
            main, rest = [
                jnp.concatenate([inverse_x[at, 0:16, :], inverse_x[at, cells_x - 16 : cells_x, :]], axis=0)
                for at in (0, 1)
            ]
            found = (
                jnp.dot(main, high[...], preferred_element_type=F32)
                + jnp.dot(main, low[...], preferred_element_type=F32)
                + jnp.dot(rest, high[...], preferred_element_type=F32)
            )
            first, last = found[0:1], found[31:32]
        else:
            for rows in halves:
                solved[comp, rows, :] = (
                    jnp.dot(inverse_x[0, rows, :], high[...], preferred_element_type=F32)
                    + jnp.dot(inverse_x[0, rows, :], low[...], preferred_element_type=F32)
                    + jnp.dot(inverse_x[1, rows, :], high[...], preferred_element_type=F32)
                )
            first, last = solved[comp, 0:1, :], solved[comp, cells_x - 1 : cells_x, :]
        edges[comp : comp + 1, :] = first
        edges[comp + 3 : comp + 4, :] = last
    edges[6:8, :] = jnp.zeros((2, cells), F32)


def chain_numbers(head, tail):
    gain = 1.0 / (1.0 - tail[-1] * head[0])
    return float(gain), float(gain * head[-1]), float(tail[-1]), float(head[0])


def ends_kernel(chain, got, edges, ends_x, sides_y, out, beside):
    gain, ratio, behind, _ = chain
    total = got[0]
    for block in range(1, got.shape[0]):
        total = total + got[block]
    total = unpack(total)
    beside[...] = padded_rows([total], 8)
    rows = []
    for end in (0, 1):
        value = jnp.sum(total * ends_x[end : end + 1, :], axis=1, keepdims=True)
        for comp in range(3):
            rows.append(
                value[comp : comp + 1] * sides_y[0:1, :] + value[comp + 3 : comp + 4] * sides_y[1:2, :]
            )
    values = edges[...] + padded_rows(rows, 8)
    links = gain * values[3:6] + (gain * ratio * behind) * values[0:3]
    out[...] = padded_rows([links, values[0:3]], 8)


def pair_kernel(chain, index, own, other, out):
    even = index[0] % 2 == 0
    first = jnp.where(even, own[...], other[...])
    second = jnp.where(even, other[...], own[...])
    out[...] = padded_rows([second[0:3] + chain[1] * first[0:3], first[3:6]], 8)


def window_kernel(chain, own, below, above, token, out):
    step = chain[1] * chain[1]
    out[...] = above[...] + step * own[...] + (step * step) * below[...]


def columns_kernel(beside, table, sides_x, token, turned, inverse, sems):
    copies = [pltpu.make_async_copy(table.at[at], inverse.at[at], sems.at[at]) for at in (0, 1)]
    for copy in copies:
        copy.start()
    high, low = split(padded_rows([beside[...]], 16))
    for copy in copies:
        copy.wait()
    lines = (
        jnp.dot(high, inverse[0], preferred_element_type=F32)
        + jnp.dot(low, inverse[0], preferred_element_type=F32)
        + jnp.dot(high, inverse[1], preferred_element_type=F32)
    )
    turned_rows(jnp.concatenate([lines[0:6], sides_x[...]], axis=0), turned)


def beside_kernel(solved, turned, sides_y, table, token, updated, inverse, high, low, sems):
    cells_x, cells_y = solved.shape[1], solved.shape[2]
    copies = [pltpu.make_async_copy(table.at[at], inverse.at[at], sems.at[at]) for at in (0, 1)]
    for copy in copies:
        copy.start()
    high[...], low[...] = split(solved[LATER])
    before = jnp.broadcast_to(sides_y[0:1, :], (8, cells_y))
    after = jnp.broadcast_to(sides_y[1:2, :], (8, cells_y))

    def step(index, carry):
        rows = pl.ds(pl.multiple_of(index * 8, 8), 8)
        here = turned[rows, :]
        for comp in range(3):
            source = updated if comp == LATER else solved
            updated[comp, rows, :] = source[comp, rows, :] + (
                here[:, comp : comp + 1] * before + here[:, comp + 3 : comp + 4] * after
            )
        return carry

    for copy in copies:
        copy.wait()
    half = cells_x // 2
    for rows in (slice(0, half), slice(half, cells_x)):
        updated[LATER, rows, :] = (
            jnp.dot(inverse[0, rows, :], high[...], preferred_element_type=F32)
            + jnp.dot(inverse[0, rows, :], low[...], preferred_element_type=F32)
            + jnp.dot(inverse[1, rows, :], high[...], preferred_element_type=F32)
        )
    lax.fori_loop(0, cells_x // 8, step, 0, unroll=4)


def final_kernel(
    chain, chips, index, own, other, pair, pair_above, far_below, far_above, turned, solved,
    out, beyond, result, sems,
):
    rows = out.shape[1]
    blocks = lane_blocks(out.shape[2])
    gain, ratio, behind, ahead = chain
    link = ratio * ratio

    even = index[0] % 2 == 0
    chip = (
        far_below[0:3, :]
        + link**3 * far_above[0:3, :]
        + (link**6 * pair_above[0:3, :] + link**7 * pair[0:3, :])
    ) * (1.0 / (1.0 - link**chips))
    before = jnp.where(even, chip, other[0:3, :] + ratio * chip)
    following = jnp.where(even, other[3:6, :], pair_above[3:6, :])
    first = (gain * behind) * own[3:6, :] + before
    last = gain * following + ahead * (own[0:3, :] + ratio * before)
    for comp in range(3):
        for side, values in enumerate((first, last)):
            wide = jnp.broadcast_to(values[comp : comp + 1, :], (8, values.shape[1]))
            for at, block in enumerate(blocks):
                beyond[3 * side + comp, at] = wide[:, block]

    def step(index, carry):
        where = pl.ds(pl.multiple_of(index * 8, 8), 8)
        here = turned[where, :]
        head = jnp.broadcast_to(here[:, 6:7], (8, 128))
        tail = jnp.broadcast_to(here[:, 7:8], (8, 128))
        for comp in range(3):
            for place, block in enumerate(blocks):
                result[comp, where, block] = solved[comp, where, block] + (
                    head * beyond[comp, place] + tail * beyond[comp + 3, place]
                )
        return carry

    stores = []
    bounds = [rows * at // 64 for at in OUT_CUTS]
    for which, (low, high) in enumerate(zip(bounds[:-1], bounds[1:])):
        lax.fori_loop(low // 8, high // 8, step, 0, unroll=4)
        store = pltpu.make_async_copy(result.at[:, low:high, :], out.at[:, low:high, :], sems.at[which])
        store.start()
        stores.append(store)
    for store in stores:
        store.wait()


VMEM = pl.BlockSpec(memory_space=pltpu.VMEM)
SMEM = pl.BlockSpec(memory_space=pltpu.SMEM)
HBM = pl.BlockSpec(memory_space=pltpu.HBM)
ANY = pl.BlockSpec(memory_space=pl.ANY)


def in_hbm(values):
    return pltpu.with_memory_space_constraint(values, pltpu.HBM)


def struct(*shape):
    return jax.ShapeDtypeStruct(shape, F32)


def call(kernel, in_specs, out_shape, scratch, flops, nbytes, **kinds):
    if "out_specs" not in kinds:
        kinds["out_specs"] = [VMEM] * len(out_shape)
    return pl.pallas_call(
        kernel,
        in_specs=in_specs,
        out_shape=out_shape,
        scratch_shapes=scratch,
        compiler_params=pltpu.CompilerParams(vmem_limit_bytes=VMEM_LIMIT),
        cost_estimate=pl.CostEstimate(flops=flops, bytes_accessed=nbytes, transcendentals=0),
        **kinds,
    )


def local(velocity, metric_first, metric_second):
    _, nx, ny = velocity.shape
    blocks_x, blocks_y = lax.axis_size("gx"), lax.axis_size("gy")
    low_x, up_x, diag_x, sig_x = coefficients(blocks_x * nx)
    low_y, up_y, diag_y, sig_y = coefficients(blocks_y * ny)
    scale = math.sqrt(sig_x * sig_y) / (diag_x * diag_y)
    inverse_x, head_x, tail_x, _ = line_tables(nx, low_x, up_x, blocks_x, True)
    inverse_y, head_y, tail_y, among_y = line_tables(ny, low_y, up_y, blocks_y, False)
    table_y = jnp.asarray(among_y.transpose(1, 0, 2, 3).reshape(blocks_y, 4 * blocks_y), F32)
    ends_x = jnp.asarray(np.stack([inverse_x[0], inverse_x[-1]]), F32)
    ends_y = jnp.asarray(np.stack([inverse_y[0], inverse_y[-1]]), F32)
    near = np.zeros((8, 32))
    for end, row in enumerate((inverse_y[0], inverse_y[-1])):
        for comp in range(3):
            near[3 * end + comp, 3 * comp : 3 * comp + 3] = row[:3]
            near[3 * end + comp, 16 + 3 * comp : 19 + 3 * comp] = row[-3:]
    near_ends = jnp.asarray(near, F32)
    sides_x = jnp.asarray(np.stack([head_x, tail_x]), F32)
    sides_y = jnp.asarray(np.stack([head_y, tail_y]), F32)
    parts_x = in_hbm(jnp.asarray(split_table(inverse_x)))
    turned_x = in_hbm(jnp.asarray(split_table(inverse_x.T)))
    parts_y = in_hbm(jnp.asarray(split_table(inverse_y.T)))
    index_x = lax.axis_index("gx").astype(jnp.int32).reshape(1)
    index_y = lax.axis_index("gy").astype(jnp.int32).reshape(1)
    m1 = metric_first.reshape(1, ny)
    m2 = metric_second.reshape(1, ny)
    cells = 3 * nx * ny
    round_x = [(i, (i + 1) % blocks_x) for i in range(blocks_x)]
    back_x = [(b, a) for a, b in round_x]
    round_y = [(i, (i + 1) % blocks_y) for i in range(blocks_y)]
    back_y = [(b, a) for a, b in round_y]

    velocity = in_hbm(velocity)
    with jax.named_scope("edges"):
        x_head, x_tail, y_head, y_tail = call(
            edges_kernel,
            [HBM],
            [struct(16, ny)] * 2 + [struct(16, nx)] * 2,
            [pltpu.VMEM((3, 8, ny), F32)] * 2
            + [pltpu.VMEM((3, nx, 128), F32)] * 2
            + [pltpu.SemaphoreType.DMA((2 + nx // 64,))],
            10 * nx * 128,
            24 * nx * 128,
        )(velocity)
    with jax.named_scope("halos"):
        before_x = lax.ppermute(x_tail, "gx", round_x)
        after_x = lax.ppermute(x_head, "gx", back_x)
        before_y = lax.ppermute(y_tail, "gy", round_y)
        after_y = lax.ppermute(y_head, "gy", back_y)
    with jax.named_scope("inner"):
        inner, ends = call(
            functools.partial(inner_kernel, scale),
            [HBM] + [VMEM] * 3,
            [struct(3, nx, ny), struct(8, nx)],
            [
                pltpu.VMEM((3, ny // 128, nx + 16, 128), F32),
                pltpu.VMEM((8, ny // 128, 8, 128), F32),
                pltpu.VMEM((6, nx, 128), F32),
                pltpu.SemaphoreType.DMA((len(CUTS) - 1, ny // 128)),
            ],
            40 * cells,
            8 * cells,
        )(velocity, m1, m2, ends_y)
    with jax.named_scope("halo_part"):
        shares_y, delta, inner = call(
            functools.partial(halo_kernel, scale),
            [SMEM, SMEM] + [VMEM] * 13 + [ANY],
            [pltpu.HBM((blocks_y, 6 * (nx // 128), 128), F32), pltpu.HBM((64, ny), F32), struct(3, nx, ny)],
            [pltpu.VMEM((blocks_y, 6 * (nx // 128), 128), F32), pltpu.VMEM((64, ny), F32)]
            + [pltpu.SemaphoreType.DMA((2,))],
            1000 * nx,
            500 * nx,
            input_output_aliases={15: 2},
            out_specs=[HBM, HBM, ANY],
        )(
            index_y, table_y, before_x, after_x, before_y, after_y, x_head, x_tail, y_head, y_tail,
            m1, m2, ends_y, near_ends, ends, inner,
        )
    with jax.named_scope("across_y"):
        got_y = lax.all_to_all(shares_y, "gy", 0, 0, tiled=True)
    with jax.named_scope("solve"):
        solved, edges = call(
            solve_kernel,
            [VMEM] + [HBM] * 3,
            [struct(3, nx, ny), struct(8, ny)],
            [pltpu.VMEM((64, ny), F32), pltpu.VMEM((2, ny, ny), BF16), pltpu.VMEM((2, nx, nx), BF16)]
            + [pltpu.VMEM((nx, ny), BF16)] * 4
            + [pltpu.VMEM((nx, 128), F32), pltpu.SemaphoreType.DMA((5,))],
            6 * cells * (nx + ny),
            8 * cells,
            input_output_aliases={0: 0},
        )(inner, in_hbm(delta), parts_y, parts_x)
    chain = chain_numbers(head_x, tail_x)
    link = struct(8, ny)
    with jax.named_scope("ends_x"):
        own, beside = call(
            functools.partial(ends_kernel, chain),
            [VMEM] * 4,
            [link, struct(8, nx)],
            [],
            100 * nx,
            500 * nx,
        )(got_y, edges, ends_x, sides_y)

    def along(values, shift):
        return lax.ppermute(values, "gx", [(i, (i + shift) % blocks_x) for i in range(blocks_x)])

    with jax.named_scope("across_x"):
        other = lax.ppermute(own, "gx", [(i, i ^ 1) for i in range(blocks_x)])
        (pair,) = call(
            functools.partial(pair_kernel, chain), [SMEM, VMEM, VMEM], [link], [], 10 * nx, 100 * nx
        )(index_x, own, other)
        pair_below = along(pair, 2)
        pair_above = along(pair, -2)
        (turned,) = call(
            columns_kernel,
            [VMEM, HBM, VMEM, VMEM],
            [struct(nx, 128)],
            [pltpu.VMEM((2, nx, nx), BF16), pltpu.SemaphoreType.DMA((2,))],
            48 * nx * nx,
            4 * nx * nx,
        )(beside, turned_x, sides_x, pair)
        (window,) = call(functools.partial(window_kernel, chain), [VMEM] * 4, [link], [], 10 * nx, 100 * nx)(
            pair, pair_below, pair_above, turned
        )
        far_below = along(window, 4)
        far_above = along(window, -6)
        (solved,) = call(
            beside_kernel,
            [VMEM] * 3 + [HBM, VMEM],
            [struct(3, nx, ny)],
            [pltpu.VMEM((2, nx, nx), BF16)]
            + [pltpu.VMEM((nx, ny), BF16)] * 2
            + [pltpu.SemaphoreType.DMA((2,))],
            2 * cells * nx,
            8 * cells,
            input_output_aliases={0: 0},
        )(solved, turned, sides_y, parts_x, window)
    with jax.named_scope("final"):
        return call(
            functools.partial(final_kernel, chain, blocks_x // 2),
            [SMEM] + [VMEM] * 8,
            struct(3, nx, ny),
            [pltpu.VMEM((6, ny // 128, 8, 128), F32), pltpu.VMEM((3, nx, ny), F32)]
            + [pltpu.SemaphoreType.DMA((len(OUT_CUTS) - 1,))],
            4 * cells,
            8 * cells,
            out_specs=ANY,
        )(index_x, own, other, pair, pair_above, far_below, far_above, turned, solved)


def solution(mesh):
    in_specs = (P(None, "gx", "gy"), P("gy"), P("gy"))
    out_specs = P(None, "gx", "gy")
    return jax.shard_map(local, mesh=mesh, in_specs=in_specs, out_specs=out_specs, check_vma=False)
```

```python
import functools
import math

import jax
import jax.numpy as jnp
import numpy as np
from jax import lax
from jax.experimental import pallas as pl
from jax.experimental.pallas import tpu as pltpu
from jax.sharding import PartitionSpec as P

VISCOSITY = 0.2
DIFFUSION = 1.0
FIRST = (45.0 / 60.0, -9.0 / 60.0, 1.0 / 60.0)
SECOND = (270.0 / 180.0, -27.0 / 180.0, 2.0 / 180.0)
CENTRE = -490.0 / 180.0
CUTS = (0, 4, 16, 64)
UNROLL = 16
LATER = 2
OUT_CUTS = (0, 4, 16, 32, 48, 64)
F32 = jnp.float32
BF16 = jnp.bfloat16
VMEM_LIMIT = 24 * 1024 * 1024


def coefficients(cells):
    sigma = cells / 4.0
    diag = 1.0 + 2.0 * DIFFUSION + sigma
    return (-(DIFFUSION + sigma) / diag, -DIFFUSION / diag, diag, sigma)


def line_tables(length, lower, upper, blocks, periodic):
    matrix = np.eye(length) + lower * np.eye(length, k=-1) + upper * np.eye(length, k=1)
    inverse = np.linalg.inv(matrix)
    head = -lower * inverse[:, 0]
    tail = -upper * inverse[:, -1]
    order = 2 * blocks
    before = np.zeros((blocks, order))
    after = np.zeros((blocks, order))
    for block in range(blocks):
        if periodic or block > 0:
            before[block, 2 * ((block - 1) % blocks) + 1] = 1.0
        if periodic or block < blocks - 1:
            after[block, 2 * ((block + 1) % blocks)] = 1.0
    system = np.eye(order)
    for block in range(blocks):
        system[2 * block] -= head[0] * before[block] + tail[0] * after[block]
        system[2 * block + 1] -= head[-1] * before[block] + tail[-1] * after[block]
    solved = np.linalg.inv(system)
    sides = np.stack([before @ solved, after @ solved], axis=1)
    sides = sides.reshape(blocks, 2, blocks, 2).transpose(0, 2, 1, 3)
    return inverse, head, tail, sides


def split(values):
    high = values.astype(BF16)
    return high, (values - high.astype(F32)).astype(BF16)


def split_table(table):
    high = np.asarray(table, np.float32).astype(BF16)
    low = (np.asarray(table, np.float64) - high.astype(np.float64)).astype(BF16)
    return np.stack([high, low])


def padded_rows(rows, count):
    filled = sum(row.shape[0] for row in rows)
    return jnp.concatenate(rows + [jnp.zeros((count - filled, rows[0].shape[1]), F32)], axis=0)


def lane_blocks(cells):
    return [slice(at, at + 128) for at in range(0, cells, 128)]


def edges_kernel(field, x_head, x_tail, y_head, y_tail, top, bottom, left, right, sems):
    rows, cells = field.shape[1], field.shape[2]
    ends = [
        pltpu.make_async_copy(field.at[:, 0:8, :], top, sems.at[0]),
        pltpu.make_async_copy(field.at[:, rows - 8 : rows, :], bottom, sems.at[1]),
    ]
    blocks = lane_blocks(rows)
    sides = [
        [
            pltpu.make_async_copy(field.at[:, block, 0:128], left.at[:, block, :], sems.at[2 + 2 * at]),
            pltpu.make_async_copy(field.at[:, block, cells - 128 : cells], right.at[:, block, :], sems.at[3 + 2 * at]),
        ]
        for at, block in enumerate(blocks)
    ]
    for group in sides + [ends]:
        for copy in group:
            copy.start()
    x_head[9:16, :] = jnp.zeros((7, cells), F32)
    x_tail[9:16, :] = jnp.zeros((7, cells), F32)
    lane = lax.broadcasted_iota(jnp.int32, (128, 128), 1)
    for group, block in zip(sides, blocks):
        for copy in group:
            copy.wait()
        packed = left[0, block, :]
        for comp in range(3):
            if comp:
                packed = jnp.where(lane < 3 * comp, packed, pltpu.roll(left[comp, block, :], 3 * comp, 1))
        packed = jnp.where(lane < 9, packed, 0.0)
        for comp in range(3):
            here = pltpu.roll(right[comp, block, :], 19 + 3 * comp, 1)
            packed = jnp.where((lane >= 16 + 3 * comp) & (lane < 19 + 3 * comp), here, packed)
        turned = packed.T
        y_head[:, block] = turned[0:16, :]
        y_tail[:, block] = turned[16:32, :]
    for copy in ends:
        copy.wait()
    for comp in range(3):
        x_head[3 * comp : 3 * comp + 3, :] = top[comp, 0:3, :]
        x_tail[3 * comp : 3 * comp + 3, :] = bottom[comp, 5:8, :]


def inner_kernel(scale, field, m1, m2, ends_y, result, ends, padded, along_rows, sums, load_sems):
    rows, cells = result.shape[1], result.shape[2]
    blocks = lane_blocks(cells)
    count = len(blocks)
    visc = scale * VISCOSITY
    zero = jnp.zeros((8, 128), F32)
    bounds = [rows * at // 64 for at in CUTS]
    spans = list(zip(bounds[:-1], bounds[1:]))
    loads = []
    for which, (first, final) in enumerate(spans):
        low, high = (first + 8 if first else 0), min(final + 8, rows)
        loads.append(
            [
                pltpu.make_async_copy(
                    field.at[:, low:high, block], padded.at[:, at, low + 8 : high + 8, :], load_sems.at[which, at]
                )
                for at, block in enumerate(blocks)
            ]
        )
    for group in loads:
        for copy in group:
            copy.start()
    for comp in range(3):
        for at in range(count):
            padded[comp, at, 0:8, :] = zero
            padded[comp, at, 8 + rows : 16 + rows, :] = zero
    slope = m1[...]
    curve = visc * slope * slope
    for at, row in enumerate(
        [scale * slope, visc * m2[...], SECOND[0] * curve, SECOND[1] * curve, SECOND[2] * curve]
        + [CENTRE * (curve + visc), ends_y[0:1, :], ends_y[1:2, :]]
    ):
        wide = jnp.broadcast_to(row, (8, cells))
        for place, block in enumerate(blocks):
            along_rows[at, place] = wide[:, block]
    lane = lax.broadcasted_iota(jnp.int32, (8, 128), 1)

    def step(index, carry):
        row = pl.multiple_of(index * 8, 8)
        fields = [[padded[comp, at, pl.ds(row + 8, 8), :] for at in range(count)] for comp in range(3)]
        along = [scale * part for part in fields[0]]
        bend = [along_rows[1, at] - fields[1][at] * along_rows[0, at] for at in range(count)]
        totals = [[along_rows[5, at] * fields[comp][at] for at in range(count)] for comp in range(3)]
        for k in (1, 2, 3):
            lead = [FIRST[k - 1] * part for part in along]
            lean = [FIRST[k - 1] * part for part in bend]
            x_ahead = [visc * SECOND[k - 1] - part for part in lead]
            x_behind = [visc * SECOND[k - 1] + part for part in lead]
            y_ahead = [along_rows[1 + k, at] + lean[at] for at in range(count)]
            y_behind = [along_rows[1 + k, at] - lean[at] for at in range(count)]
            for comp in range(3):
                left = [pltpu.roll(part, 128 - k, 1) for part in fields[comp]] + [zero]
                right = [zero] + [pltpu.roll(part, k, 1) for part in fields[comp]]
                for at in range(count):
                    totals[comp][at] = (
                        totals[comp][at]
                        + (
                            x_ahead[at] * padded[comp, at, pl.ds(row + 8 + k, 8), :]
                            + x_behind[at] * padded[comp, at, pl.ds(row + 8 - k, 8), :]
                        )
                        + (
                            y_ahead[at] * jnp.where(lane < 128 - k, left[at], left[at + 1])
                            + y_behind[at] * jnp.where(lane >= k, right[at + 1], right[at])
                        )
                    )
        for comp in range(3):
            for end in (0, 1):
                value = totals[comp][0] * along_rows[6 + end, 0]
                for at in range(1, count):
                    value = value + totals[comp][at] * along_rows[6 + end, at]
                sums[3 * end + comp, pl.ds(row, 8), :] = value
            for at, block in enumerate(blocks):
                result[comp, pl.ds(row, 8), block] = totals[comp][at]
        return carry

    for which, (first, final) in enumerate(spans):
        for copy in loads[which]:
            copy.wait()
        lax.fori_loop(first // 8, final // 8, step, 0, unroll=min(UNROLL, (final - first) // 8))
    for block in lane_blocks(rows):
        values = [jnp.sum(sums[at, block, :].T, axis=0, keepdims=True) for at in range(6)]
        ends[:, block] = padded_rows(values, 8)


def pack(values):
    return jnp.concatenate([values[0:6, block] for block in lane_blocks(values.shape[1])], axis=0)


def unpack(values):
    count = values.shape[0] // 6
    return jnp.concatenate([values[6 * at : 6 * at + 6, :] for at in range(count)], axis=1)


def write_shares(table, index, values, shares):
    swapped = pack(jnp.concatenate([values[3:6], values[0:3]], axis=0))
    values = pack(values)
    place = lax.broadcasted_iota(jnp.int32, values.shape, 0)
    third = jnp.zeros(values.shape, jnp.bool_)
    for at in range(0, values.shape[0], 6):
        third = third | ((place >= at) & (place < at + 3))
    for other in range(shares.shape[0]):
        base = 4 * other
        straight = jnp.where(third, table[index[0], base], table[index[0], base + 3])
        crossed = jnp.where(third, table[index[0], base + 1], table[index[0], base + 2])
        shares[other] = straight * values + crossed * swapped


def edge_lines(shape):
    rows = lax.broadcasted_iota(jnp.int32, shape, 0)
    line = rows - 3 * ((rows >= 3).astype(jnp.int32) + (rows >= 6).astype(jnp.int32))
    return rows, jnp.where(rows < 9, line, 3)


def halo_sides(before, after, curves, bends_head, bends_tail):
    _, line = edge_lines(before.shape)
    head = tail = None
    for k in (1, 2, 3):
        a, b = FIRST[k - 1], SECOND[k - 1]
        low = jnp.where(line < k, b * curves[0] - a * bends_head, 0.0)
        high = jnp.where((line >= 3 - k) & (line < 3), b * curves[1] + a * bends_tail, 0.0)
        low = low * (pltpu.roll(before, 16 - (3 - k), 0) if k < 3 else before)
        high = high * (pltpu.roll(after, 3 - k, 0) if k < 3 else after)
        head = low if head is None else head + low
        tail = high if tail is None else tail + high
    return head, tail


def tiled_lines(lines):
    return jnp.concatenate([lines, lines, lines, jnp.zeros((7, lines.shape[1]), F32)], axis=0)


def halo_kernel(
    scale, index, table, before_x, after_x, before_y, after_y, x_head, x_tail, y_head, y_tail,
    m1, m2, ends_y, near_ends, ends, inner, shares, delta, kept, near_shares, near_delta, sems,
):
    cells_x = before_y.shape[1]
    cells_y = before_x.shape[1]
    visc = scale * VISCOSITY
    head_x, tail_x = halo_sides(
        before_x[...],
        after_x[...],
        (visc, visc),
        -scale * tiled_lines(x_head[0:3, :]),
        -scale * tiled_lines(x_tail[0:3, :]),
    )
    first, last = slice(0, 128), slice(cells_y - 128, cells_y)
    near = padded_rows([m1[:, first], m1[:, last], m2[:, first], m2[:, last]], 128).T
    spread = [
        tiled_lines(jnp.broadcast_to(near[lines, at : at + 1], (3, cells_x)))
        for at, lines in enumerate((slice(0, 3), slice(125, 128), slice(0, 3), slice(125, 128)))
    ]
    slopes = spread[0:2]
    offsets = [visc * offset for offset in spread[2:4]]
    bends = [
        offsets[side] - (scale * slopes[side]) * tiled_lines(lines[3:6, :])
        for side, lines in enumerate((y_head, y_tail))
    ]
    head_y, tail_y = halo_sides(
        jnp.where(index[0] > 0, before_y[...], 0.0),
        jnp.where(index[0] < shares.shape[0] - 1, after_y[...], 0.0),
        [visc * slope * slope for slope in slopes],
        bends[0],
        bends[1],
    )
    for at, part in enumerate((head_x, tail_x, head_y, tail_y)):
        near_delta[16 * at : 16 * at + 16, :] = part
    store = pltpu.make_async_copy(near_delta, delta, sems.at[0])
    store.start()
    values = ends[...] + lax.dot_general(
        near_ends[...],
        jnp.concatenate([head_y, tail_y], axis=0),
        (((1,), (0,)), ((), ())),
        precision=lax.Precision.HIGHEST,
        preferred_element_type=F32,
    )
    rows, line = edge_lines((16, 128))
    lane = lax.broadcasted_iota(jnp.int32, (16, 128), 1)
    extra = []
    for end in (0, 1):
        weights = ends_y[end : end + 1, :]
        first = jnp.sum(head_x * weights, axis=1, keepdims=True) * jnp.where(lane == line, 1.0, 0.0)
        final = jnp.sum(tail_x * weights, axis=1, keepdims=True) * jnp.where(lane == line + 125, 1.0, 0.0)
        for comp in range(3):
            own = (rows >= 3 * comp) & (rows < 3 * comp + 3)
            extra.append(
                jnp.concatenate(
                    [
                        jnp.sum(jnp.where(own, first, 0.0), axis=0, keepdims=True),
                        jnp.zeros((1, cells_x - 256), F32),
                        jnp.sum(jnp.where(own, final, 0.0), axis=0, keepdims=True),
                    ],
                    axis=1,
                )
            )
    write_shares(table, index, values + padded_rows(extra, 8), near_shares)
    leave = pltpu.make_async_copy(near_shares, shares, sems.at[1])
    leave.start()
    store.wait()
    leave.wait()


def turned_rows(rows, turned):
    tall = jnp.concatenate([rows, jnp.zeros((128 - rows.shape[0], rows.shape[1]), F32)], axis=0)
    for block in lane_blocks(rows.shape[1]):
        turned[block, :] = tall[:, block].T


def solve_kernel(
    inner, delta, table_y, table_x, solved, edges,
    near_delta, inverse_y, inverse_x, above, below, high, low, turned, sems,
):
    cells_x, cells = solved.shape[1], solved.shape[2]
    tables_y = [pltpu.make_async_copy(table_y.at[at], inverse_y.at[at], sems.at[at]) for at in (0, 1)]
    tables_x = [pltpu.make_async_copy(table_x.at[at], inverse_x.at[at], sems.at[2 + at]) for at in (0, 1)]
    sides = pltpu.make_async_copy(delta, near_delta, sems.at[4])
    for copy in [sides] + tables_y + tables_x:
        copy.start()
    sides.wait()
    turned_rows(near_delta[32:64, :], turned)
    lane = lax.broadcasted_iota(jnp.int32, (128, 128), 1)
    half = cells_x // 2
    halves = (slice(0, half), slice(half, cells_x))
    for comp in range(3):
        for block in lane_blocks(cells_x):
            tile = turned[block, :]
            near = pltpu.roll(tile, 128 - 3 * comp, 1) if comp else tile
            far = pltpu.roll(tile, 109 - 3 * comp, 1)
            full = jnp.concatenate(
                [
                    inner[comp, block, 0:128] + jnp.where(lane < 3, near, 0.0),
                    inner[comp, block, 128 : cells - 128],
                    inner[comp, block, cells - 128 : cells] + jnp.where(lane >= 125, far, 0.0),
                ],
                axis=1,
            )
            if block.start == 0:
                full = full + padded_rows([near_delta[3 * comp : 3 * comp + 3, :]], 128)
            if block.stop == cells_x:
                full = full + jnp.concatenate(
                    [jnp.zeros((125, cells), F32), near_delta[16 + 3 * comp : 19 + 3 * comp, :]], axis=0
                )
            above[block, :], below[block, :] = split(full)
        if comp == 0:
            for copy in tables_y:
                copy.wait()
        for rows in halves:
            found = (
                jnp.dot(above[rows, :], inverse_y[0], preferred_element_type=F32)
                + jnp.dot(below[rows, :], inverse_y[0], preferred_element_type=F32)
                + jnp.dot(above[rows, :], inverse_y[1], preferred_element_type=F32)
            )
            high[rows, :], low[rows, :] = split(found)
            if comp == LATER:
                solved[comp, rows, :] = found
        if comp == 0:
            for copy in tables_x:
                copy.wait()
        if comp == LATER:
            main, rest = [
                jnp.concatenate([inverse_x[at, 0:16, :], inverse_x[at, cells_x - 16 : cells_x, :]], axis=0)
                for at in (0, 1)
            ]
            found = (
                jnp.dot(main, high[...], preferred_element_type=F32)
                + jnp.dot(main, low[...], preferred_element_type=F32)
                + jnp.dot(rest, high[...], preferred_element_type=F32)
            )
            first, last = found[0:1], found[31:32]
        else:
            for rows in halves:
                solved[comp, rows, :] = (
                    jnp.dot(inverse_x[0, rows, :], high[...], preferred_element_type=F32)
                    + jnp.dot(inverse_x[0, rows, :], low[...], preferred_element_type=F32)
                    + jnp.dot(inverse_x[1, rows, :], high[...], preferred_element_type=F32)
                )
            first, last = solved[comp, 0:1, :], solved[comp, cells_x - 1 : cells_x, :]
        edges[comp : comp + 1, :] = first
        edges[comp + 3 : comp + 4, :] = last
    edges[6:8, :] = jnp.zeros((2, cells), F32)


def chain_numbers(head, tail):
    gain = 1.0 / (1.0 - tail[-1] * head[0])
    return float(gain), float(gain * head[-1]), float(tail[-1]), float(head[0])


def ends_kernel(chain, got, edges, ends_x, sides_y, out, beside):
    gain, ratio, behind, _ = chain
    total = got[0]
    for block in range(1, got.shape[0]):
        total = total + got[block]
    total = unpack(total)
    beside[...] = padded_rows([total], 8)
    rows = []
    for end in (0, 1):
        value = jnp.sum(total * ends_x[end : end + 1, :], axis=1, keepdims=True)
        for comp in range(3):
            rows.append(
                value[comp : comp + 1] * sides_y[0:1, :] + value[comp + 3 : comp + 4] * sides_y[1:2, :]
            )
    values = edges[...] + padded_rows(rows, 8)
    links = gain * values[3:6] + (gain * ratio * behind) * values[0:3]
    out[...] = padded_rows([links, values[0:3]], 8)


def pair_kernel(chain, index, own, other, out):
    even = index[0] % 2 == 0
    first = jnp.where(even, own[...], other[...])
    second = jnp.where(even, other[...], own[...])
    out[...] = padded_rows([second[0:3] + chain[1] * first[0:3], first[3:6]], 8)


def window_kernel(chain, own, below, above, token, out):
    step = chain[1] * chain[1]
    out[...] = above[...] + step * own[...] + (step * step) * below[...]


def columns_kernel(beside, table, sides_x, token, turned, inverse, sems):
    copies = [pltpu.make_async_copy(table.at[at], inverse.at[at], sems.at[at]) for at in (0, 1)]
    for copy in copies:
        copy.start()
    high, low = split(padded_rows([beside[...]], 16))
    for copy in copies:
        copy.wait()
    lines = (
        jnp.dot(high, inverse[0], preferred_element_type=F32)
        + jnp.dot(low, inverse[0], preferred_element_type=F32)
        + jnp.dot(high, inverse[1], preferred_element_type=F32)
    )
    turned_rows(jnp.concatenate([lines[0:6], sides_x[...]], axis=0), turned)


def beside_kernel(solved, turned, sides_y, table, token, updated, inverse, high, low, sems):
    cells_x, cells_y = solved.shape[1], solved.shape[2]
    copies = [pltpu.make_async_copy(table.at[at], inverse.at[at], sems.at[at]) for at in (0, 1)]
    for copy in copies:
        copy.start()
    high[...], low[...] = split(solved[LATER])
    before = jnp.broadcast_to(sides_y[0:1, :], (8, cells_y))
    after = jnp.broadcast_to(sides_y[1:2, :], (8, cells_y))

    def step(comps, index, carry):
        rows = pl.ds(pl.multiple_of(index * 8, 8), 8)
        here = turned[rows, :]
        for comp in comps:
            source = updated if comp == LATER else solved
            updated[comp, rows, :] = source[comp, rows, :] + (
                here[:, comp : comp + 1] * before + here[:, comp + 3 : comp + 4] * after
            )
        return carry

    others = [comp for comp in range(3) if comp != LATER]
    lax.fori_loop(0, cells_x // 8, functools.partial(step, others), 0, unroll=4)
    for copy in copies:
        copy.wait()
    half = cells_x // 2
    for rows in (slice(0, half), slice(half, cells_x)):
        updated[LATER, rows, :] = (
            jnp.dot(inverse[0, rows, :], high[...], preferred_element_type=F32)
            + jnp.dot(inverse[0, rows, :], low[...], preferred_element_type=F32)
            + jnp.dot(inverse[1, rows, :], high[...], preferred_element_type=F32)
        )
    lax.fori_loop(0, cells_x // 8, functools.partial(step, [LATER]), 0, unroll=4)


def final_kernel(
    chain, chips, index, own, other, pair, pair_above, far_below, far_above, turned, solved,
    out, beyond, result, sems,
):
    rows = out.shape[1]
    blocks = lane_blocks(out.shape[2])
    gain, ratio, behind, ahead = chain
    link = ratio * ratio

    even = index[0] % 2 == 0
    chip = (
        far_below[0:3, :]
        + link**3 * far_above[0:3, :]
        + (link**6 * pair_above[0:3, :] + link**7 * pair[0:3, :])
    ) * (1.0 / (1.0 - link**chips))
    before = jnp.where(even, chip, other[0:3, :] + ratio * chip)
    following = jnp.where(even, other[3:6, :], pair_above[3:6, :])
    first = (gain * behind) * own[3:6, :] + before
    last = gain * following + ahead * (own[0:3, :] + ratio * before)
    for comp in range(3):
        for side, values in enumerate((first, last)):
            wide = jnp.broadcast_to(values[comp : comp + 1, :], (8, values.shape[1]))
            for at, block in enumerate(blocks):
                beyond[3 * side + comp, at] = wide[:, block]

    def step(index, carry):
        where = pl.ds(pl.multiple_of(index * 8, 8), 8)
        here = turned[where, :]
        head = jnp.broadcast_to(here[:, 6:7], (8, 128))
        tail = jnp.broadcast_to(here[:, 7:8], (8, 128))
        for comp in range(3):
            for place, block in enumerate(blocks):
                result[comp, where, block] = solved[comp, where, block] + (
                    head * beyond[comp, place] + tail * beyond[comp + 3, place]
                )
        return carry

    stores = []
    bounds = [rows * at // 64 for at in OUT_CUTS]
    for which, (low, high) in enumerate(zip(bounds[:-1], bounds[1:])):
        lax.fori_loop(low // 8, high // 8, step, 0, unroll=4)
        store = pltpu.make_async_copy(result.at[:, low:high, :], out.at[:, low:high, :], sems.at[which])
        store.start()
        stores.append(store)
    for store in stores:
        store.wait()


VMEM = pl.BlockSpec(memory_space=pltpu.VMEM)
SMEM = pl.BlockSpec(memory_space=pltpu.SMEM)
HBM = pl.BlockSpec(memory_space=pltpu.HBM)
ANY = pl.BlockSpec(memory_space=pl.ANY)


def in_hbm(values):
    return pltpu.with_memory_space_constraint(values, pltpu.HBM)


def struct(*shape):
    return jax.ShapeDtypeStruct(shape, F32)


def call(kernel, in_specs, out_shape, scratch, flops, nbytes, **kinds):
    if "out_specs" not in kinds:
        kinds["out_specs"] = [VMEM] * len(out_shape)
    return pl.pallas_call(
        kernel,
        in_specs=in_specs,
        out_shape=out_shape,
        scratch_shapes=scratch,
        compiler_params=pltpu.CompilerParams(vmem_limit_bytes=VMEM_LIMIT),
        cost_estimate=pl.CostEstimate(flops=flops, bytes_accessed=nbytes, transcendentals=0),
        **kinds,
    )


def local(velocity, metric_first, metric_second):
    _, nx, ny = velocity.shape
    blocks_x, blocks_y = lax.axis_size("gx"), lax.axis_size("gy")
    low_x, up_x, diag_x, sig_x = coefficients(blocks_x * nx)
    low_y, up_y, diag_y, sig_y = coefficients(blocks_y * ny)
    scale = math.sqrt(sig_x * sig_y) / (diag_x * diag_y)
    inverse_x, head_x, tail_x, _ = line_tables(nx, low_x, up_x, blocks_x, True)
    inverse_y, head_y, tail_y, among_y = line_tables(ny, low_y, up_y, blocks_y, False)
    table_y = jnp.asarray(among_y.transpose(1, 0, 2, 3).reshape(blocks_y, 4 * blocks_y), F32)
    ends_x = jnp.asarray(np.stack([inverse_x[0], inverse_x[-1]]), F32)
    ends_y = jnp.asarray(np.stack([inverse_y[0], inverse_y[-1]]), F32)
    near = np.zeros((8, 32))
    for end, row in enumerate((inverse_y[0], inverse_y[-1])):
        for comp in range(3):
            near[3 * end + comp, 3 * comp : 3 * comp + 3] = row[:3]
            near[3 * end + comp, 16 + 3 * comp : 19 + 3 * comp] = row[-3:]
    near_ends = jnp.asarray(near, F32)
    sides_x = jnp.asarray(np.stack([head_x, tail_x]), F32)
    sides_y = jnp.asarray(np.stack([head_y, tail_y]), F32)
    parts_x = in_hbm(jnp.asarray(split_table(inverse_x)))
    turned_x = in_hbm(jnp.asarray(split_table(inverse_x.T)))
    parts_y = in_hbm(jnp.asarray(split_table(inverse_y.T)))
    index_x = lax.axis_index("gx").astype(jnp.int32).reshape(1)
    index_y = lax.axis_index("gy").astype(jnp.int32).reshape(1)
    m1 = metric_first.reshape(1, ny)
    m2 = metric_second.reshape(1, ny)
    cells = 3 * nx * ny
    round_x = [(i, (i + 1) % blocks_x) for i in range(blocks_x)]
    back_x = [(b, a) for a, b in round_x]
    round_y = [(i, (i + 1) % blocks_y) for i in range(blocks_y)]
    back_y = [(b, a) for a, b in round_y]

    velocity = in_hbm(velocity)
    with jax.named_scope("edges"):
        x_head, x_tail, y_head, y_tail = call(
            edges_kernel,
            [HBM],
            [struct(16, ny)] * 2 + [struct(16, nx)] * 2,
            [pltpu.VMEM((3, 8, ny), F32)] * 2
            + [pltpu.VMEM((3, nx, 128), F32)] * 2
            + [pltpu.SemaphoreType.DMA((2 + nx // 64,))],
            10 * nx * 128,
            24 * nx * 128,
        )(velocity)
    with jax.named_scope("halos"):
        before_x = lax.ppermute(x_tail, "gx", round_x)
        after_x = lax.ppermute(x_head, "gx", back_x)
        before_y = lax.ppermute(y_tail, "gy", round_y)
        after_y = lax.ppermute(y_head, "gy", back_y)
    with jax.named_scope("inner"):
        inner, ends = call(
            functools.partial(inner_kernel, scale),
            [HBM] + [VMEM] * 3,
            [struct(3, nx, ny), struct(8, nx)],
            [
                pltpu.VMEM((3, ny // 128, nx + 16, 128), F32),
                pltpu.VMEM((8, ny // 128, 8, 128), F32),
                pltpu.VMEM((6, nx, 128), F32),
                pltpu.SemaphoreType.DMA((len(CUTS) - 1, ny // 128)),
            ],
            40 * cells,
            8 * cells,
        )(velocity, m1, m2, ends_y)
    with jax.named_scope("halo_part"):
        shares_y, delta, inner = call(
            functools.partial(halo_kernel, scale),
            [SMEM, SMEM] + [VMEM] * 13 + [ANY],
            [pltpu.HBM((blocks_y, 6 * (nx // 128), 128), F32), pltpu.HBM((64, ny), F32), struct(3, nx, ny)],
            [pltpu.VMEM((blocks_y, 6 * (nx // 128), 128), F32), pltpu.VMEM((64, ny), F32)]
            + [pltpu.SemaphoreType.DMA((2,))],
            1000 * nx,
            500 * nx,
            input_output_aliases={15: 2},
            out_specs=[HBM, HBM, ANY],
        )(
            index_y, table_y, before_x, after_x, before_y, after_y, x_head, x_tail, y_head, y_tail,
            m1, m2, ends_y, near_ends, ends, inner,
        )
    with jax.named_scope("across_y"):
        got_y = lax.all_to_all(shares_y, "gy", 0, 0, tiled=True)
    with jax.named_scope("solve"):
        solved, edges = call(
            solve_kernel,
            [VMEM] + [HBM] * 3,
            [struct(3, nx, ny), struct(8, ny)],
            [pltpu.VMEM((64, ny), F32), pltpu.VMEM((2, ny, ny), BF16), pltpu.VMEM((2, nx, nx), BF16)]
            + [pltpu.VMEM((nx, ny), BF16)] * 4
            + [pltpu.VMEM((nx, 128), F32), pltpu.SemaphoreType.DMA((5,))],
            6 * cells * (nx + ny),
            8 * cells,
            input_output_aliases={0: 0},
        )(inner, in_hbm(delta), parts_y, parts_x)
    chain = chain_numbers(head_x, tail_x)
    link = struct(8, ny)
    with jax.named_scope("ends_x"):
        own, beside = call(
            functools.partial(ends_kernel, chain),
            [VMEM] * 4,
            [link, struct(8, nx)],
            [],
            100 * nx,
            500 * nx,
        )(got_y, edges, ends_x, sides_y)

    def along(values, shift):
        return lax.ppermute(values, "gx", [(i, (i + shift) % blocks_x) for i in range(blocks_x)])

    with jax.named_scope("across_x"):
        other = lax.ppermute(own, "gx", [(i, i ^ 1) for i in range(blocks_x)])
        (pair,) = call(
            functools.partial(pair_kernel, chain), [SMEM, VMEM, VMEM], [link], [], 10 * nx, 100 * nx
        )(index_x, own, other)
        pair_below = along(pair, 2)
        pair_above = along(pair, -2)
        (turned,) = call(
            columns_kernel,
            [VMEM, HBM, VMEM, VMEM],
            [struct(nx, 128)],
            [pltpu.VMEM((2, nx, nx), BF16), pltpu.SemaphoreType.DMA((2,))],
            48 * nx * nx,
            4 * nx * nx,
        )(beside, turned_x, sides_x, pair)
        (window,) = call(functools.partial(window_kernel, chain), [VMEM] * 4, [link], [], 10 * nx, 100 * nx)(
            pair, pair_below, pair_above, turned
        )
        far_below = along(window, 4)
        far_above = along(window, -6)
        (solved,) = call(
            beside_kernel,
            [VMEM] * 3 + [HBM, VMEM],
            [struct(3, nx, ny)],
            [pltpu.VMEM((2, nx, nx), BF16)]
            + [pltpu.VMEM((nx, ny), BF16)] * 2
            + [pltpu.SemaphoreType.DMA((2,))],
            2 * cells * nx,
            8 * cells,
            input_output_aliases={0: 0},
        )(solved, turned, sides_y, parts_x, window)
    with jax.named_scope("final"):
        return call(
            functools.partial(final_kernel, chain, blocks_x // 2),
            [SMEM] + [VMEM] * 8,
            struct(3, nx, ny),
            [pltpu.VMEM((6, ny // 128, 8, 128), F32), pltpu.VMEM((3, nx, ny), F32)]
            + [pltpu.SemaphoreType.DMA((len(OUT_CUTS) - 1,))],
            4 * cells,
            8 * cells,
            out_specs=ANY,
        )(index_x, own, other, pair, pair_above, far_below, far_above, turned, solved)


def solution(mesh):
    in_specs = (P(None, "gx", "gy"), P("gy"), P("gy"))
    out_specs = P(None, "gx", "gy")
    return jax.shard_map(local, mesh=mesh, in_specs=in_specs, out_specs=out_specs, check_vma=False)
```
